256 devices in a mesh: sub: 8 (over x, z_hi), ifc: 32 (over z_lo, y, core).
Axes of the slice: x: 4, y: 4, z: 8 (z_hi: 2, z_lo: 4; z = z_hi * 4 + z_lo), core: 2. Of those that a mesh axis runs over, the one named last changes fastest.
Arguments:
- stretch_store: bfloat16 [8, 32, 512, 1024], P('sub', 'ifc'), may hold values from -6 to 6
- stretch_owner: int32 [8, 2], P('sub'), may hold values from 0 to 31, as said below
- tile_map: int32 [8, 64, 2, 8], P('sub', 'ifc'), may hold values from 0 to 4
- inverse_block: bfloat16 [8, 64, 1024, 1024], P('sub', 'ifc'), may hold values from -0.1875 to 0.1875
- face_coupling: bfloat16 [8, 64, 1024, 128], P('sub', 'ifc'), may hold values from -0.1875 to 0.1875
- row_offset: int32 [8, 64], P('sub', 'ifc'), may hold values from 0 to 4064, as said below
- row_count: int32 [8, 64], P('sub', 'ifc'), may hold values from 32 to 128, as said below
- interface_block: float32 [4096, 2048], P('ifc', 'sub'), may hold values from -6 to 6
Outputs:
- schur: float32 [4096, 2048], P('ifc', 'sub')
The draws below stay inside these ranges and needn't reach their ends.
Inputs may be any that keep to these rules, and one draw needn't show every extreme that they name: `stretch_owner`: the two owners of one sub index differ. With p = j // 2, the subdomain at index j of the second dimension starts between max(0, p * 128 - 128 // 2) and p * 128 + 128 // 2, and row_offset + row_count <= min(4096, (p + 2) * 128). `row_count`: some subdomain has exactly 128 rows.
All inputs are finite; a program needn't handle non-finite values.
Results may differ from the reference program's by a relative error of at most 0.0027.
Values may be sent and summed in bfloat16 or wider, within the bound.
A program may use at most 64 MiB of HBM per device.

```python
import jax
import jax.numpy as jnp
from jax import lax

W = 1024
NI = 1024
TR = 128
NT = 4
SPD = 2
RO = 128
NTI = 8
CR = 512
NGW = 4096
N_SUB = 8
N_IFC = 32


def draw_spans(key):
    first, second, third = jax.random.split(key, 3)
    columns_all = SPD * N_IFC
    count = jax.random.randint(first, (N_SUB * columns_all,), RO // 4, RO + 1, dtype=jnp.int32)
    marked = jax.random.randint(second, (), 0, N_SUB * columns_all, dtype=jnp.int32)
    count = count.at[marked].set(RO).reshape(N_SUB, columns_all)
    column = (jnp.arange(columns_all, dtype=jnp.int32) // SPD)[None, :]
    jitter = jax.random.randint(third, (N_SUB, columns_all), -(RO // 2), RO // 2 + 1, dtype=jnp.int32)
    offset = jnp.clip(column * RO + jitter, 0, RO * N_IFC - count)
    return (offset, count)


def draw_row_offset(key, part):
    spans = draw_spans(key)
    return spans[0]


def draw_row_count(key, part):
    spans = draw_spans(key)
    return spans[1]


def draw_stretch_owner(key, part):
    key = jax.random.fold_in(key, 13)
    first, second, third = jax.random.split(key, 3)
    leader = jax.random.randint(first, (N_SUB,), 0, N_IFC, dtype=jnp.int32)
    step_size = jax.random.randint(second, (N_SUB,), 1, N_IFC, dtype=jnp.int32)
    marked = jax.random.randint(third, (), 0, N_SUB, dtype=jnp.int32)
    leader = leader.at[marked].set(N_IFC - 1)
    step_size = step_size.at[marked].set(1)
    follower = (leader + step_size) % N_IFC
    return jnp.stack([leader, follower], axis=1)


def set_ends(entries, stream_key, least, largest):
    extent = entries.shape
    spot = [jax.random.randint(jax.random.fold_in(stream_key, axis), (), 0, extent[axis]) for axis in range(len(extent))]
    entries = entries.at[tuple(spot)].set(least)
    longest = extent.index(max(extent))
    spot[longest] = (spot[longest] + 1) % extent[longest]
    return entries.at[tuple(spot)].set(largest)


def shard_levels(own_key, shape, cuts, low, high):
    factor_of = 1.0
    for axis_at, shards_of in cuts:
        steps = jax.random.uniform(jax.random.fold_in(jax.random.fold_in(own_key, 6), axis_at), (shards_of,), jnp.float32, low / len(cuts), high / len(cuts))
        factor_of = factor_of * jnp.repeat(jnp.exp(steps), shape[axis_at] // shards_of).reshape((-1,) + (1,) * (len(shape) - 1 - axis_at))
    return factor_of


def centred(stream_key, shape, spread, reach, cuts=(), held_as=jnp.bfloat16):
    values = spread * jax.random.normal(stream_key, shape, jnp.float32)
    if cuts:
        values = values * shard_levels(stream_key, shape, cuts, -0.22, 0.18)
    return jnp.clip(values, -reach, reach).astype(held_as)


def setup_inputs(seed: int = 0) -> dict:
    keys = jax.random.split(jax.random.key(seed), 9)
    return {
        "stretch_store": centred(keys[0], (N_SUB, N_IFC, CR, W), 1.0, 6.0, ((0, 8), (1, 32))),
        "stretch_owner": draw_stretch_owner(jax.random.fold_in(keys[8], 71), 0),
        "tile_map": set_ends(jax.random.randint(keys[2], (N_SUB, SPD * N_IFC, 2, NTI), 0, NT + 1), jax.random.fold_in(keys[2], 1), 0, NT).astype(jnp.int32),
        "inverse_block": centred(keys[3], (N_SUB, SPD * N_IFC, NI, NI), NI ** -0.5, 0.1875, ((0, 8), (1, 32))),
        "face_coupling": centred(keys[4], (N_SUB, SPD * N_IFC, NI, RO), NI ** -0.5, 0.1875, ((0, 8), (1, 32))),
        "row_offset": draw_row_offset(jax.random.fold_in(keys[8], 71), 0),
        "row_count": draw_row_count(jax.random.fold_in(keys[8], 71), 0),
        "interface_block": centred(keys[7], (NGW, 2 * W), 1.0, 6.0, ((0, 32), (1, 8)), jnp.float32),
    }


def reference(stretch_store, stretch_owner, tile_map, inverse_block, face_coupling, row_offset, row_count, interface_block):
    columns_all = SPD * N_IFC

    def one_subdomain(position, total):
        s = (position // columns_all).astype(jnp.int32)
        j = (position % columns_all).astype(jnp.int32)
        pieces = []
        for k in range(2):
            owner_now = stretch_owner[s, k]
            tile_rows = stretch_store[s, owner_now].reshape(NT, TR, W).astype(jnp.float32)
            onehot = (tile_map[s, j, k][:, None] == jnp.arange(NT, dtype=jnp.int32)[None, :]).astype(jnp.float32)
            picked = jnp.einsum("it,trw->irw", onehot, tile_rows).reshape(NI, W)
            pieces.append(picked.astype(jnp.bfloat16))
        coupling = jnp.concatenate(pieces, axis=1)
        solved = jnp.dot(inverse_block[s, j], coupling, preferred_element_type=jnp.float32).astype(jnp.bfloat16)
        partial_value = jnp.dot(face_coupling[s, j].T, solved, preferred_element_type=jnp.float32)
        live_rows = jnp.arange(RO, dtype=jnp.int32)[:, None] < row_count[s, j]
        partial_value = jnp.where(live_rows, partial_value, jnp.float32(0.0))
        offset_now = row_offset[s, j].astype(jnp.int32)
        zero_col = jnp.zeros((), jnp.int32)
        current = lax.dynamic_slice(total, (offset_now, zero_col), (RO, 2 * W))
        return lax.dynamic_update_slice(total, current + partial_value, (offset_now, zero_col))

    total = jnp.zeros((NGW + RO, 2 * W), jnp.float32)
    total = lax.fori_loop(0, N_SUB * columns_all, one_subdomain, total)
    return interface_block - total[:NGW]
```

```python
import jax
import jax.numpy as jnp
from jax import lax
from jax.experimental import pallas as pl
from jax.experimental.pallas import tpu as pltpu
from jax.sharding import PartitionSpec as P

MESH = pl.DeviceIdType.MESH
F32 = jnp.float32
BF16 = jnp.bfloat16
NT_DIMS = (((1,), (1,)), ((), ()))


def aligned(value, unit):
    return pl.multiple_of(value, unit)


def kernel(
    owner_ref,
    map_ref,
    offset_ref,
    count_ref,
    store_ref,
    inverse_ref,
    face_ref,
    iface_ref,
    out_ref,
    st,
    inv,
    face,
    iface,
    r1_first,
    r1_second,
    s2,
    r2,
    m2,
    r3,
    m3,
    r4,
    bmat,
    placed,
    gband,
    band,
    nb,
    hs,
    hf,
    pmat,
    late,
    cross,
    load_sem,
    s1_send,
    s1_recv,
    s2_send,
    s2_recv,
    s3_send,
    s3_recv,
    s4_send,
    s4_recv,
    s5_send,
    s5_recv,
    s6_send,
    s6_recv,
    nb_send,
    nb_recv,
    h_send,
    h_recv,
    late_send,
    late_recv,
):
    sub = lax.axis_index("sub")
    ifc = lax.axis_index("ifc")
    x, zh = sub // 2, sub % 2
    zl, y, c = ifc // 8, (ifc // 2) % 4, ifc % 2

    def flip(value, mask):
        out = 0
        for bit in (1, 2):
            digit = (value // bit) % 2
            out = out + bit * ((1 - digit) if mask & bit else digit)
        return out

    def device(x_, zh_, zl_, y_, c_):
        return (x_ * 2 + zh_, zl_ * 8 + y_ * 2 + c_)

    oc = 1 - c
    r1 = (r1_first, r1_second)
    first_partner = (flip(y, 1), flip(y, 3))
    second_partner = (flip(y, 3), flip(y, 1))
    y0, y1 = y % 2, y // 2
    half = ((y0 + y1) % 2, y1)
    quarter = (y1, y0)

    partners = [device(x, zh, zl, y, oc)]
    for h in range(2):
        for core in (c, oc):
            partners.append(device(x, zh, zl, first_partner[h], core))
    for a in range(4):
        for b in range(4):
            if a or b:
                partners.append(device(flip(x, a), zh, flip(zl, b), y, c))
    for a in range(1, 4):
        partners.append(device(flip(x, a), zh, zl, y, oc))
    before, after = lax.rem(ifc + 31, 32), lax.rem(ifc + 1, 32)
    partners.append((sub, before))
    partners.append((sub, after))
    for core in (c, oc):
        partners.append(device(x, 1 - zh, zl, y, core))
    barrier = pltpu.get_barrier_semaphore()
    for partner in partners:
        pl.semaphore_signal(barrier, inc=1, device_id=partner, device_id_type=MESH)

    loads = []
    face_load = pltpu.make_async_copy(face_ref.at[0], face, load_sem.at[0])
    face_load.start()
    inv_loads = []
    for l in range(2):
        cp = pltpu.make_async_copy(inverse_ref.at[0, l], inv.at[l], load_sem.at[1 + l])
        cp.start()
        inv_loads.append(cp)
    n = 3
    for j in range(2):
        for xh in range(2):
            for cc in range(2):
                cp = pltpu.make_async_copy(
                    store_ref.at[0, 0, :, pl.ds(xh * 512 + j * 256 + cc * 128, 128)],
                    st.at[j, xh, cc],
                    load_sem.at[n],
                )
                cp.start()
                loads.append(cp)
                n += 1
    iface_load = pltpu.make_async_copy(iface_ref, iface, load_sem.at[n])
    iface_load.start()

    face_load.wait()
    row_at = lax.broadcasted_iota(jnp.int32, (256, 128), 0)
    col_at = lax.broadcasted_iota(jnp.int32, (256, 128), 1)
    for l in range(2):
        start = offset_ref[0, l] - (ifc * 128 - 64)
        here = jnp.logical_and(row_at == col_at + start, col_at < count_ref[0, l])
        place = jnp.where(here, 1.0, 0.0).astype(BF16)
        placed[l] = lax.dot_general(
            place, face[l], NT_DIMS, preferred_element_type=F32
        ).astype(BF16)
    for l in range(2):
        inv_loads[l].wait()

        def columns(i, _):
            at = pl.ds(aligned(i * 256, 256), 256)
            gband[l, :, at] = jnp.dot(
                placed[l], inv[l, :, at], preferred_element_type=F32
            )
            return 0

        lax.fori_loop(0, 4, columns, 0)

    def fold(r, _):
        rows = pl.ds(aligned(r * 64, 64), 64)
        for k in range(2):
            for t in range(4):
                acc = jnp.zeros((64, 128), F32)
                for l in range(2):
                    for i in range(8):
                        weight = jnp.where(map_ref[0, l, k, i] == t, 1.0, 0.0)
                        acc = acc + weight * gband[l, rows, i * 128 : (i + 1) * 128]
                at = k * 512 + t * 128
                band[rows, at : at + 128] = acc
        return 0

    lax.fori_loop(0, 4, fold, 0)

    for cp in loads:
        cp.wait()
    steps = ((1 - zh), zh)
    for n in range(2):
        for h in range(2):
            rows = pl.ds(aligned(h * 256 + half[h] * 128, 128), 128)
            r1[n][h, 0] = st[steps[n], :, c, rows, :]
            r1[n][h, 4] = jnp.zeros((2, 128, 128), BF16)

    picks = []
    for h in range(2):
        row = []
        for k in range(2):
            o = owner_ref[0, k]
            pick = jnp.int32(4)
            sources = (
                zl * 8 + y * 2 + c,
                zl * 8 + y * 2 + oc,
                zl * 8 + first_partner[h] * 2 + c,
                zl * 8 + first_partner[h] * 2 + oc,
            )
            for at, source in enumerate(sources):
                pick = jnp.where(o == source, at, pick)
            row.append(pick)
        picks.append(row)

    started = []

    def send(src, dst, send_sem, recv_sem, to):
        cp = pltpu.make_async_remote_copy(
            src_ref=src,
            dst_ref=dst,
            send_sem=send_sem,
            recv_sem=recv_sem,
            device_id=to,
            device_id_type=MESH,
        )
        cp.start()
        started.append(cp)
        return cp

    pl.semaphore_wait(barrier, len(partners))

    def stage1(n):
        cps = []
        for h in range(2):
            rows = pl.ds(aligned(h * 256 + (1 - half[h]) * 128, 128), 128)
            for d, core in enumerate((c, oc)):
                cps.append(
                    send(
                        st.at[steps[n], :, core, rows, :],
                        r1[n].at[h, 2 + d],
                        s1_send.at[n, h, d],
                        s1_recv.at[n, h, d],
                        device(x, zh, zl, first_partner[h], core),
                    )
                )
            rows = pl.ds(aligned(h * 256 + half[h] * 128, 128), 128)
            cps.append(
                send(
                    st.at[steps[n], :, oc, rows, :],
                    r1[n].at[h, 1],
                    s1_send.at[n, h, 2],
                    s1_recv.at[n, h, 2],
                    device(x, zh, zl, y, oc),
                )
            )
        return cps

    def stage2(n, cps):
        out = []
        for cp in cps:
            cp.wait_recv()
        for h in range(2):
            rows = pl.ds(aligned((1 - quarter[h]) * 64, 64), 64)
            for k in range(2):
                s2[n, h, 2 * k : 2 * k + 2] = r1[n][h, picks[h][k], :, rows, :]
            out.append(
                send(
                    s2.at[n, h],
                    r2.at[n, h],
                    s2_send.at[n, h],
                    s2_recv.at[n, h],
                    device(x, zh, zl, second_partner[h], c),
                )
            )
        return out

    def stage3(n, cps):
        out = []
        for cp in cps:
            cp.wait_recv()
        for h in range(2):
            rows = pl.ds(aligned(quarter[h] * 64, 64), 64)
            for k in range(2):
                m2[n, h, 2 * k : 2 * k + 2] = (
                    r1[n][h, picks[h][k], :, rows, :] + r2[n, h, 2 * k : 2 * k + 2]
                )
        for d in range(1, 4):
            to = flip(zl, d)
            out.append(
                send(
                    m2.at[n, :, :, pl.ds(aligned(to * 16, 16), 16), :],
                    r3.at[n, d],
                    s3_send.at[n, d],
                    s3_recv.at[n, d],
                    device(x, zh, to, y, c),
                )
            )
        return out

    def stage4(n, cps):
        out = []
        for cp in cps:
            cp.wait_recv()
        rows = pl.ds(aligned(zl * 16, 16), 16)
        m3[n] = m2[n, :, :, rows, :] + r3[n, 1] + r3[n, 2] + r3[n, 3]
        for a in range(4):
            for b in range(4):
                if a or b:
                    out.append(
                        send(
                            m3.at[n, :, flip(x, a)],
                            r4.at[n, x, :, rows, :],
                            s4_send.at[n, a, b],
                            s4_recv.at[n, a, b],
                            device(flip(x, a), zh, flip(zl, b), y, c),
                        )
                    )
        r4[n, x, :, rows, :] = m3[n, :, x]
        return out

    def stage5(n, cps):
        out = []
        for cp in cps:
            cp.wait_recv()
        for h in range(2):
            rows = pl.ds(aligned(h * 256 + half[h] * 128 + quarter[h] * 64, 64), 64)
            out.append(
                send(
                    r4.at[n, :, h],
                    bmat.at[n, :, rows, :],
                    s5_send.at[n, h],
                    s5_recv.at[n, h],
                    device(x, zh, zl, second_partner[h], c),
                )
            )
            bmat[n, :, rows, :] = r4[n, :, h]
        return out

    def stage6(n, cps):
        out = []
        for cp in cps:
            cp.wait_recv()
        for h in range(2):
            rows = pl.ds(aligned(h * 256 + half[h] * 128, 128), 128)
            out.append(
                send(
                    bmat.at[n, :, rows, :],
                    bmat.at[n, :, rows, :],
                    s6_send.at[n, h],
                    s6_recv.at[n, h],
                    device(x, zh, zl, first_partner[h], c),
                )
            )
        return out

    def product(n, cps):
        for cp in cps:
            cp.wait_recv()
        total = jnp.zeros((256, 128), F32)
        for at in range(4):
            total = total + jnp.dot(hf[at], bmat[n, at], preferred_element_type=F32)
        pmat[n] = total

    a1 = stage1(0)
    nb_cps = [
        send(band.at[0:64], nb.at[1], nb_send.at[0], nb_recv.at[0], (sub, before)),
        send(band.at[192:256], nb.at[0], nb_send.at[1], nb_recv.at[1], (sub, after)),
    ]
    b1 = stage1(1)
    a2 = stage2(0, a1)

    for cp in nb_cps:
        cp.wait_recv()
    for k in range(2):
        at = slice(k * 512, (k + 1) * 512)
        hs[k, 0:64] = (band[64:128, at] + nb[0, :, at]).astype(BF16)
        hs[k, 64:128] = (band[128:192, at] + nb[1, :, at]).astype(BF16)
    own_rows = pl.ds(aligned(c * 128, 128), 128)
    h_cps = []
    for a in range(4):
        for d, core in enumerate((c, oc)):
            if a or d:
                h_cps.append(
                    send(
                        hs.at[flip(x, a) // 2],
                        hf.at[x, own_rows, :],
                        h_send.at[a, d],
                        h_recv.at[a, d],
                        device(flip(x, a), zh, zl, y, core),
                    )
                )
    hf[x, own_rows, :] = hs[x // 2]

    b2 = stage2(1, b1)
    a3 = stage3(0, a2)
    b3 = stage3(1, b2)
    a4 = stage4(0, a3)
    b4 = stage4(1, b3)
    a5 = stage5(0, a4)
    b5 = stage5(1, b4)
    a6 = stage6(0, a5)
    b6 = stage6(1, b5)
    for cp in h_cps:
        cp.wait_recv()
    product(0, a6)
    late_cps = []
    for d, core in enumerate((c, oc)):
        late_cps.append(
            send(
                pmat.at[0, pl.ds(aligned(core * 128, 128), 128), :],
                late.at[d],
                late_send.at[d],
                late_recv.at[d],
                device(x, 1 - zh, zl, y, core),
            )
        )
    product(1, b6)
    late_cps.append(
        send(
            pmat.at[1, pl.ds(aligned(oc * 128, 128), 128), :],
            cross,
            late_send.at[2],
            late_recv.at[2],
            device(x, zh, zl, y, oc),
        )
    )
    iface_load.wait()
    for cp in late_cps:
        cp.wait_recv()
    own = pl.ds(aligned(c * 128, 128), 128)
    other = pl.ds(aligned(oc * 128, 128), 128)
    out_ref[:, own] = iface[:, own] - (pmat[1, own, :] + late[0])
    out_ref[:, other] = iface[:, other] - (cross[...] + late[1])
    for cp in started:
        cp.wait_send()


def per_device(
    stretch_store,
    stretch_owner,
    tile_map,
    inverse_block,
    face_coupling,
    row_offset,
    row_count,
    interface_block,
):
    smem = pl.BlockSpec(memory_space=pltpu.SMEM)
    anywhere = pl.BlockSpec(memory_space=pl.ANY)
    dma = pltpu.SemaphoreType.DMA
    return pl.pallas_call(
        kernel,
        out_shape=jax.ShapeDtypeStruct((128, 256), F32),
        in_specs=[smem] * 4 + [anywhere] * 4,
        out_specs=pl.BlockSpec(memory_space=pltpu.VMEM),
        scratch_shapes=[
            pltpu.VMEM((2, 2, 2, 512, 128), BF16),
            pltpu.VMEM((2, 1024, 1024), BF16),
            pltpu.VMEM((2, 1024, 128), BF16),
            pltpu.VMEM((128, 256), F32),
            pltpu.VMEM((2, 5, 2, 128, 128), BF16),
            pltpu.VMEM((2, 5, 2, 128, 128), BF16),
            pltpu.VMEM((2, 2, 4, 64, 128), BF16),
            pltpu.VMEM((2, 2, 4, 64, 128), BF16),
            pltpu.VMEM((2, 2, 4, 64, 128), BF16),
            pltpu.VMEM((2, 4, 2, 4, 16, 128), BF16),
            pltpu.VMEM((2, 2, 4, 16, 128), BF16),
            pltpu.VMEM((2, 4, 2, 64, 128), BF16),
            pltpu.VMEM((2, 4, 512, 128), BF16),
            pltpu.VMEM((2, 256, 1024), BF16),
            pltpu.VMEM((2, 256, 1024), F32),
            pltpu.VMEM((256, 1024), F32),
            pltpu.VMEM((2, 64, 1024), F32),
            pltpu.VMEM((2, 128, 512), BF16),
            pltpu.VMEM((4, 256, 512), BF16),
            pltpu.VMEM((2, 256, 128), F32),
            pltpu.VMEM((2, 128, 128), F32),
            pltpu.VMEM((128, 128), F32),
            dma((12,)),
            dma((2, 2, 3)),
            dma((2, 2, 3)),
            dma((2, 2)),
            dma((2, 2)),
            dma((2, 4)),
            dma((2, 4)),
            dma((2, 4, 4)),
            dma((2, 4, 4)),
            dma((2, 2)),
            dma((2, 2)),
            dma((2, 2)),
            dma((2, 2)),
            dma((2,)),
            dma((2,)),
            dma((4, 2)),
            dma((4, 2)),
            dma((3,)),
            dma((3,)),
        ],
        compiler_params=pltpu.CompilerParams(
            collective_id=0, has_side_effects=True, vmem_limit_bytes=40 * 1024 * 1024
        ),
        name="schur",
    )(
        stretch_owner,
        tile_map,
        row_offset,
        row_count,
        stretch_store,
        inverse_block,
        face_coupling,
        interface_block,
    )


def solution(mesh):
    return jax.shard_map(
        per_device,
        mesh=mesh,
        in_specs=(
            P("sub", "ifc", None, None),
            P("sub", None),
            P("sub", "ifc", None, None),
            P("sub", "ifc", None, None),
            P("sub", "ifc", None, None),
            P("sub", "ifc"),
            P("sub", "ifc"),
            P("ifc", "sub"),
        ),
        out_specs=P("ifc", "sub"),
        check_vma=False,
    )
```

```python
import jax
import jax.numpy as jnp
from jax import lax
from jax.experimental import pallas as pl
from jax.experimental.pallas import tpu as pltpu
from jax.sharding import PartitionSpec as P

MESH = pl.DeviceIdType.MESH
F32 = jnp.float32
BF16 = jnp.bfloat16
NT_DIMS = (((1,), (1,)), ((), ()))


def aligned(value, unit):
    return pl.multiple_of(value, unit)


def kernel(
    owner_hbm,
    map_hbm,
    offset_hbm,
    count_hbm,
    store_ref,
    inverse_ref,
    face_ref,
    iface_ref,
    out_ref,
    owner_ref,
    map_ref,
    offset_ref,
    count_ref,
    st,
    inv,
    face,
    iface,
    r1_first,
    r1_second,
    so,
    s2,
    r2,
    m2,
    r3,
    m3,
    r4,
    bmat,
    placed,
    gband,
    band,
    nb,
    hs,
    low,
    hf,
    pmat,
    away,
    late,
    cross,
    load_sem,
    s0_send,
    s0_recv,
    s1_send,
    s1_recv,
    s2_send,
    s2_recv,
    s3_send,
    s3_recv,
    s4_send,
    s4_recv,
    s5_send,
    s5_recv,
    s6_send,
    s6_recv,
    nb_send,
    nb_recv,
    h_send,
    h_recv,
    late_send,
    late_recv,
):
    sub = lax.axis_index("sub")
    ifc = lax.axis_index("ifc")
    x, zh = sub // 2, sub % 2
    zl, y, c = ifc // 8, (ifc // 2) % 4, ifc % 2

    def flip(value, mask):
        out = 0
        for bit in (1, 2):
            digit = (value // bit) % 2
            out = out + bit * ((1 - digit) if mask & bit else digit)
        return out

    def device(x_, zh_, zl_, y_, c_):
        return (x_ * 2 + zh_, zl_ * 8 + y_ * 2 + c_)

    oc = 1 - c
    r1 = (r1_first, r1_second)
    first_partner = (flip(y, 1), flip(y, 3))
    second_partner = (flip(y, 3), flip(y, 1))
    y0, y1 = y % 2, y // 2
    half = ((y0 + y1) % 2, y1)
    quarter = (y1, y0)

    partners = [device(x, zh, zl, y, oc)]
    for h in range(2):
        partners.append(device(x, zh, zl, first_partner[h], c))
    for a in range(4):
        for b in range(4):
            if a or b:
                partners.append(device(flip(x, a), zh, flip(zl, b), y, c))
    before, after = lax.rem(ifc + 31, 32), lax.rem(ifc + 1, 32)
    partners.append((sub, before))
    partners.append((sub, after))
    for core in (c, oc):
        partners.append(device(x, 1 - zh, zl, y, core))
    barrier = pltpu.get_barrier_semaphore()
    for partner in partners:
        pl.semaphore_signal(barrier, inc=1, device_id=partner, device_id_type=MESH)

    scalar_loads = []
    for at, (src, dst) in enumerate(
        (
            (owner_hbm, owner_ref),
            (map_hbm, map_ref),
            (offset_hbm, offset_ref),
            (count_hbm, count_ref),
        )
    ):
        cp = pltpu.make_async_copy(src, dst, load_sem.at[12 + at])
        cp.start()
        scalar_loads.append(cp)
    loads = []
    face_load = pltpu.make_async_copy(face_ref.at[0], face, load_sem.at[0])
    face_load.start()
    inv_loads = []
    for l in range(2):
        cp = pltpu.make_async_copy(inverse_ref.at[0, l], inv.at[l], load_sem.at[1 + l])
        cp.start()
        inv_loads.append(cp)
    n = 3
    for j in range(2):
        for xh in range(2):
            for cc in range(2):
                cp = pltpu.make_async_copy(
                    store_ref.at[0, 0, :, pl.ds(xh * 512 + j * 256 + cc * 128, 128)],
                    st.at[j, xh, cc],
                    load_sem.at[n],
                )
                cp.start()
                loads.append(cp)
                n += 1
    iface_load = pltpu.make_async_copy(iface_ref, iface, load_sem.at[n])
    iface_load.start()

    def place_rows():
        face_load.wait()
        row_at = lax.broadcasted_iota(jnp.int32, (256, 128), 0)
        col_at = lax.broadcasted_iota(jnp.int32, (256, 128), 1)
        for l in range(2):
            start = offset_ref[0, l] - (ifc * 128 - 64)
            here = jnp.logical_and(row_at == col_at + start, col_at < count_ref[0, l])
            place = jnp.where(here, 1.0, 0.0).astype(BF16)
            placed[l] = lax.dot_general(
                place, face[l], NT_DIMS, preferred_element_type=F32
            ).astype(BF16)

    def apply_inverse():
        for l in range(2):
            inv_loads[l].wait()

            def columns(i, _):
                at = pl.ds(aligned(i * 256, 256), 256)
                gband[l, :, at] = jnp.dot(
                    placed[l], inv[l, :, at], preferred_element_type=F32
                )
                return 0

            lax.fori_loop(0, 4, columns, 0)

    def fold_tiles():
        def fold(r, _):
            rows = pl.ds(aligned(r * 64, 64), 64)
            for k in range(2):
                for t in range(4):
                    acc = jnp.zeros((64, 128), F32)
                    for l in range(2):
                        for i in range(8):
                            weight = jnp.where(map_ref[0, l, k, i] == t, 1.0, 0.0)
                            acc = acc + weight * gband[l, rows, i * 128 : (i + 1) * 128]
                    at = k * 512 + t * 128
                    band[rows, at : at + 128] = acc
            return 0

        lax.fori_loop(0, 4, fold, 0)

    for cp in loads:
        cp.wait()
    steps = ((1 - zh), zh)
    def kept(h):
        return pl.ds(aligned(h * 256 + half[h] * 128, 128), 128)

    def given(h):
        return pl.ds(aligned(h * 256 + (1 - half[h]) * 128, 128), 128)

    def own_blocks(n):
        for h in range(2):
            r1[n][h, 0] = st[steps[n], :, c, kept(h), :]
            r1[n][h, 4] = jnp.zeros((2, 128, 128), BF16)

    started = []

    def send(src, dst, send_sem, recv_sem, to):
        cp = pltpu.make_async_remote_copy(
            src_ref=src,
            dst_ref=dst,
            send_sem=send_sem,
            recv_sem=recv_sem,
            device_id=to,
            device_id_type=MESH,
        )
        cp.start()
        started.append(cp)
        return cp

    got = []

    def arrive(cps):
        for cp in cps:
            cp.wait_recv()
            got.append(cp)

    pl.semaphore_wait(barrier, len(partners))

    def to_other_core(n):
        out = []
        for h in range(2):
            out.append(
                send(
                    st.at[steps[n], :, oc, given(h), :],
                    so.at[n, h],
                    s0_send.at[n, h],
                    s0_recv.at[n, h],
                    device(x, zh, zl, y, oc),
                )
            )
        return out

    def stage1(n):
        out = []
        for h in range(2):
            out.append(
                send(
                    st.at[steps[n], :, c, given(h), :],
                    r1[n].at[h, 2],
                    s1_send.at[n, h, 0],
                    s1_recv.at[n, h, 0],
                    device(x, zh, zl, first_partner[h], c),
                )
            )
        return out

    def stage1_rest(n, cps):
        out = []
        arrive(cps)
        for h in range(2):
            out.append(
                send(
                    so.at[n, h],
                    r1[n].at[h, 3],
                    s1_send.at[n, h, 1],
                    s1_recv.at[n, h, 1],
                    device(x, zh, zl, first_partner[h], c),
                )
            )
        for h in range(2):
            out.append(
                send(
                    st.at[steps[n], :, oc, kept(h), :],
                    r1[n].at[h, 1],
                    s1_send.at[n, h, 2],
                    s1_recv.at[n, h, 2],
                    device(x, zh, zl, y, oc),
                )
            )
        return out

    def stage2(n, cps):
        out = []
        arrive(cps)
        for h in range(2):
            rows = pl.ds(aligned((1 - quarter[h]) * 64, 64), 64)
            for k in range(2):
                s2[n, h, 2 * k : 2 * k + 2] = r1[n][h, picks[h][k], :, rows, :]
            out.append(
                send(
                    s2.at[n, h],
                    r2.at[n, h],
                    s2_send.at[n, h],
                    s2_recv.at[n, h],
                    device(x, zh, zl, second_partner[h], c),
                )
            )
        return out

    def stage3(n, cps):
        out = []
        arrive(cps)
        for h in range(2):
            rows = pl.ds(aligned(quarter[h] * 64, 64), 64)
            for k in range(2):
                m2[n, h, 2 * k : 2 * k + 2] = (
                    r1[n][h, picks[h][k], :, rows, :] + r2[n, h, 2 * k : 2 * k + 2]
                )
        for d in range(1, 4):
            to = flip(zl, d)
            out.append(
                send(
                    m2.at[n, :, :, pl.ds(aligned(to * 16, 16), 16), :],
                    r3.at[n, d],
                    s3_send.at[n, d],
                    s3_recv.at[n, d],
                    device(x, zh, to, y, c),
                )
            )
        return out

    def stage4(n, cps):
        out = []
        arrive(cps)
        rows = pl.ds(aligned(zl * 16, 16), 16)
        m3[n] = m2[n, :, :, rows, :] + r3[n, 1] + r3[n, 2] + r3[n, 3]
        for a in range(4):
            for b in range(4):
                if a or b:
                    out.append(
                        send(
                            m3.at[n, :, flip(x, a)],
                            r4.at[n, x, :, rows, :],
                            s4_send.at[n, a, b],
                            s4_recv.at[n, a, b],
                            device(flip(x, a), zh, flip(zl, b), y, c),
                        )
                    )
        r4[n, x, :, rows, :] = m3[n, :, x]
        return out

    def stage5(n, cps):
        out = []
        arrive(cps)
        for h in range(2):
            rows = pl.ds(aligned(h * 256 + half[h] * 128 + quarter[h] * 64, 64), 64)
            out.append(
                send(
                    r4.at[n, :, h],
                    bmat.at[n, :, rows, :],
                    s5_send.at[n, h],
                    s5_recv.at[n, h],
                    device(x, zh, zl, second_partner[h], c),
                )
            )
            bmat[n, :, rows, :] = r4[n, :, h]
        return out

    def stage6(n, cps):
        out = []
        arrive(cps)
        for h in range(2):
            rows = pl.ds(aligned(h * 256 + half[h] * 128, 128), 128)
            out.append(
                send(
                    bmat.at[n, :, rows, :],
                    bmat.at[n, :, rows, :],
                    s6_send.at[n, h],
                    s6_recv.at[n, h],
                    device(x, zh, zl, first_partner[h], c),
                )
            )
        return out

    def product(n, cps):
        arrive(cps)
        total = jnp.zeros((256, 128), F32)
        for at in range(4):
            total = total + jnp.dot(hf[at], bmat[n, at], preferred_element_type=F32)
        total = total + jnp.dot(hf[4], bmat[n, x], preferred_element_type=F32)
        pmat[n] = total

    a0 = to_other_core(0)
    a1 = stage1(0)
    a1 += stage1_rest(0, a0)
    own_blocks(0)
    for cp in scalar_loads:
        cp.wait()
    picks = []
    for h in range(2):
        row = []
        for k in range(2):
            o = owner_ref[0, k]
            pick = jnp.int32(4)
            sources = (
                zl * 8 + y * 2 + c,
                zl * 8 + y * 2 + oc,
                zl * 8 + first_partner[h] * 2 + c,
                zl * 8 + first_partner[h] * 2 + oc,
            )
            for at, source in enumerate(sources):
                pick = jnp.where(o == source, at, pick)
            row.append(pick)
        picks.append(row)

    place_rows()
    apply_inverse()
    a2 = stage2(0, a1)
    b0 = to_other_core(1)
    b1 = stage1(1)
    b1 += stage1_rest(1, b0)
    own_blocks(1)
    fold_tiles()
    a3 = stage3(0, a2)
    nb_cps = [
        send(band.at[0:64], nb.at[1], nb_send.at[0], nb_recv.at[0], (sub, before)),
        send(band.at[192:256], nb.at[0], nb_send.at[1], nb_recv.at[1], (sub, after)),
    ]
    b2 = stage2(1, b1)
    a4 = stage4(0, a3)
    b3 = stage3(1, b2)

    arrive(nb_cps)
    for k in range(2):
        at = slice(k * 512, (k + 1) * 512)
        for part in range(2):
            rows = slice(part * 64, (part + 1) * 64)
            full = band[64 + part * 64 : 128 + part * 64, at] + nb[part, :, at]
            high = full.astype(BF16)
            hs[k, rows] = high
            low[k, rows] = (full - high.astype(F32)).astype(BF16)
    own_rows = pl.ds(aligned(c * 128, 128), 128)
    h_cps = []
    for a in range(1, 4):
        h_cps.append(
            send(
                hs.at[flip(x, a) // 2],
                hf.at[x, own_rows, :],
                h_send.at[a],
                h_recv.at[a],
                device(flip(x, a), zh, zl, y, c),
            )
        )
    hf[x, own_rows, :] = hs[x // 2]
    hf[4, own_rows, :] = low[x // 2]

    b4 = stage4(1, b3)
    a5 = stage5(0, a4)
    a6 = stage6(0, a5)
    b5 = stage5(1, b4)
    arrive(h_cps)
    h_cps = [
        send(
            hf.at[:, own_rows, :],
            hf.at[:, own_rows, :],
            h_send.at[0],
            h_recv.at[0],
            device(x, zh, zl, y, oc),
        )
    ]
    arrive(h_cps)
    product(0, a6)
    away[...] = pmat[0].astype(BF16)
    late_cps = []
    for d, core in enumerate((c, oc)):
        late_cps.append(
            send(
                away.at[pl.ds(aligned(core * 128, 128), 128), :],
                late.at[d],
                late_send.at[d],
                late_recv.at[d],
                device(x, 1 - zh, zl, y, core),
            )
        )
    b6 = stage6(1, b5)
    product(1, b6)
    late_cps.append(
        send(
            pmat.at[1, pl.ds(aligned(oc * 128, 128), 128), :],
            cross,
            late_send.at[2],
            late_recv.at[2],
            device(x, zh, zl, y, oc),
        )
    )
    iface_load.wait()
    arrive(late_cps)
    own = pl.ds(aligned(c * 128, 128), 128)
    other = pl.ds(aligned(oc * 128, 128), 128)
    out_ref[:, own] = iface[:, own] - (pmat[1, own, :] + late[0].astype(F32))
    out_ref[:, other] = iface[:, other] - (cross[...] + late[1].astype(F32))
    for cp in started:
        cp.wait_send()


def per_device(
    stretch_store,
    stretch_owner,
    tile_map,
    inverse_block,
    face_coupling,
    row_offset,
    row_count,
    interface_block,
):
    hbm = pl.BlockSpec(memory_space=pltpu.HBM)
    dma = pltpu.SemaphoreType.DMA
    return pl.pallas_call(
        kernel,
        out_shape=jax.ShapeDtypeStruct((128, 256), F32),
        in_specs=[hbm] * 8,
        out_specs=pl.BlockSpec(memory_space=pltpu.VMEM),
        scratch_shapes=[
            pltpu.SMEM((1, 2), jnp.int32),
            pltpu.SMEM((1, 2, 2, 8), jnp.int32),
            pltpu.SMEM((1, 2), jnp.int32),
            pltpu.SMEM((1, 2), jnp.int32),
            pltpu.VMEM((2, 2, 2, 512, 128), BF16),
            pltpu.VMEM((2, 1024, 1024), BF16),
            pltpu.VMEM((2, 1024, 128), BF16),
            pltpu.VMEM((128, 256), F32),
            pltpu.VMEM((2, 5, 2, 128, 128), BF16),
            pltpu.VMEM((2, 5, 2, 128, 128), BF16),
            pltpu.VMEM((2, 2, 2, 128, 128), BF16),
            pltpu.VMEM((2, 2, 4, 64, 128), BF16),
            pltpu.VMEM((2, 2, 4, 64, 128), BF16),
            pltpu.VMEM((2, 2, 4, 64, 128), BF16),
            pltpu.VMEM((2, 4, 2, 4, 16, 128), BF16),
            pltpu.VMEM((2, 2, 4, 16, 128), BF16),
            pltpu.VMEM((2, 4, 2, 64, 128), BF16),
            pltpu.VMEM((2, 4, 512, 128), BF16),
            pltpu.VMEM((2, 256, 1024), BF16),
            pltpu.VMEM((2, 256, 1024), F32),
            pltpu.VMEM((256, 1024), F32),
            pltpu.VMEM((2, 64, 1024), F32),
            pltpu.VMEM((2, 128, 512), BF16),
            pltpu.VMEM((2, 128, 512), BF16),
            pltpu.VMEM((5, 256, 512), BF16),
            pltpu.VMEM((2, 256, 128), F32),
            pltpu.VMEM((256, 128), BF16),
            pltpu.VMEM((2, 128, 128), BF16),
            pltpu.VMEM((128, 128), F32),
            dma((16,)),
            dma((2, 2)),
            dma((2, 2)),
            dma((2, 2, 3)),
            dma((2, 2, 3)),
            dma((2, 2)),
            dma((2, 2)),
            dma((2, 4)),
            dma((2, 4)),
            dma((2, 4, 4)),
            dma((2, 4, 4)),
            dma((2, 2)),
            dma((2, 2)),
            dma((2, 2)),
            dma((2, 2)),
            dma((2,)),
            dma((2,)),
            dma((4,)),
            dma((4,)),
            dma((3,)),
            dma((3,)),
        ],
        compiler_params=pltpu.CompilerParams(
            collective_id=0, has_side_effects=True, vmem_limit_bytes=60 * 1024 * 1024
        ),
        name="schur",
    )(
        stretch_owner,
        tile_map,
        row_offset,
        row_count,
        stretch_store,
        inverse_block,
        face_coupling,
        interface_block,
    )


def solution(mesh):
    return jax.shard_map(
        per_device,
        mesh=mesh,
        in_specs=(
            P("sub", "ifc", None, None),
            P("sub", None),
            P("sub", "ifc", None, None),
            P("sub", "ifc", None, None),
            P("sub", "ifc", None, None),
            P("sub", "ifc"),
            P("sub", "ifc"),
            P("ifc", "sub"),
        ),
        out_specs=P("ifc", "sub"),
        check_vma=False,
    )
```

```python
import jax
import jax.numpy as jnp
from jax import lax
from jax.experimental import pallas as pl
from jax.experimental.pallas import tpu as pltpu
from jax.sharding import PartitionSpec as P

MESH = pl.DeviceIdType.MESH
F32 = jnp.float32
BF16 = jnp.bfloat16
NT_DIMS = (((1,), (1,)), ((), ()))


def aligned(value, unit):
    return pl.multiple_of(value, unit)


def kernel(
    owner_hbm,
    map_hbm,
    offset_hbm,
    count_hbm,
    store_ref,
    inverse_ref,
    face_ref,
    iface_ref,
    out_ref,
    owner_ref,
    map_ref,
    offset_ref,
    count_ref,
    st,
    inv,
    face,
    iface,
    r1_first,
    r1_second,
    so,
    s2,
    r2,
    m2,
    r3,
    m3,
    r4,
    bmat,
    placed,
    gband,
    band,
    nb,
    hs,
    low,
    hf,
    pmat,
    away,
    away_sum,
    late,
    cross,
    load_sem,
    s0_send,
    s0_recv,
    s1_send,
    s1_recv,
    s2_send,
    s2_recv,
    s3_send,
    s3_recv,
    s4_send,
    s4_recv,
    s5_send,
    s5_recv,
    s6_send,
    s6_recv,
    nb_send,
    nb_recv,
    h_send,
    h_recv,
    late_send,
    late_recv,
):
    sub = lax.axis_index("sub")
    ifc = lax.axis_index("ifc")
    x, zh = sub // 2, sub % 2
    zl, y, c = ifc // 8, (ifc // 2) % 4, ifc % 2

    def flip(value, mask):
        out = 0
        for bit in (1, 2):
            digit = (value // bit) % 2
            out = out + bit * ((1 - digit) if mask & bit else digit)
        return out

    def device(x_, zh_, zl_, y_, c_):
        return (x_ * 2 + zh_, zl_ * 8 + y_ * 2 + c_)

    oc = 1 - c
    r1 = (r1_first, r1_second)
    first_partner = (flip(y, 1), flip(y, 3))
    second_partner = (flip(y, 3), flip(y, 1))
    y0, y1 = y % 2, y // 2
    half = ((y0 + y1) % 2, y1)
    quarter = (y1, y0)

    partners = [device(x, zh, zl, y, oc)]
    for h in range(2):
        partners.append(device(x, zh, zl, first_partner[h], c))
    for a in range(4):
        for b in range(4):
            if a or b:
                partners.append(device(flip(x, a), zh, flip(zl, b), y, c))
    before, after = lax.rem(ifc + 31, 32), lax.rem(ifc + 1, 32)
    partners.append((sub, before))
    partners.append((sub, after))
    partners.append(device(x, 1 - zh, zl, y, c))
    steps = ((1 - zh), zh)
    strips = ([], [])

    def load_strips(n):
        for xh in range(2):
            for cc in range(2):
                at = aligned(xh * 512 + steps[n] * 256 + cc * 128, 128)
                cp = pltpu.make_async_copy(
                    store_ref.at[0, 0, :, pl.ds(at, 128)],
                    st.at[n, xh, cc],
                    load_sem.at[n * 4 + xh * 2 + cc],
                )
                cp.start()
                strips[n].append(cp)

    load_strips(0)
    barrier = pltpu.get_barrier_semaphore()
    for partner in partners:
        pl.semaphore_signal(barrier, inc=1, device_id=partner, device_id_type=MESH)

    load_strips(1)
    scalar_loads = []
    for at, (src, dst) in enumerate(
        (
            (owner_hbm, owner_ref),
            (map_hbm, map_ref),
            (offset_hbm, offset_ref),
            (count_hbm, count_ref),
        )
    ):
        cp = pltpu.make_async_copy(src, dst, load_sem.at[8 + at])
        cp.start()
        scalar_loads.append(cp)
    face_load = pltpu.make_async_copy(face_ref.at[0], face, load_sem.at[12])
    face_load.start()
    inv_loads = []
    for l in range(2):
        cp = pltpu.make_async_copy(inverse_ref.at[0, l], inv.at[l], load_sem.at[13 + l])
        cp.start()
        inv_loads.append(cp)
    iface_load = pltpu.make_async_copy(iface_ref, iface, load_sem.at[15])
    iface_load.start()

    def place_rows():
        face_load.wait()
        row_at = lax.broadcasted_iota(jnp.int32, (256, 128), 0)
        col_at = lax.broadcasted_iota(jnp.int32, (256, 128), 1)
        for l in range(2):
            start = offset_ref[0, l] - (ifc * 128 - 64)
            here = jnp.logical_and(row_at == col_at + start, col_at < count_ref[0, l])
            place = jnp.where(here, 1.0, 0.0).astype(BF16)
            placed[l] = lax.dot_general(
                place, face[l], NT_DIMS, preferred_element_type=F32
            ).astype(BF16)

    def apply_inverse():
        for l in range(2):
            inv_loads[l].wait()

            def columns(i, _):
                at = pl.ds(aligned(i * 256, 256), 256)
                gband[l, :, at] = jnp.dot(
                    placed[l], inv[l, :, at], preferred_element_type=F32
                )
                return 0

            lax.fori_loop(0, 4, columns, 0)

    def fold_tiles():
        def fold(r, _):
            rows = pl.ds(aligned(r * 64, 64), 64)
            for k in range(2):
                for t in range(4):
                    acc = jnp.zeros((64, 128), F32)
                    for l in range(2):
                        for i in range(8):
                            weight = jnp.where(map_ref[0, l, k, i] == t, 1.0, 0.0)
                            acc = acc + weight * gband[l, rows, i * 128 : (i + 1) * 128]
                    at = k * 512 + t * 128
                    band[rows, at : at + 128] = acc
            return 0

        lax.fori_loop(0, 4, fold, 0)

    def kept(h):
        return pl.ds(aligned(h * 256 + half[h] * 128, 128), 128)

    def given(h):
        return pl.ds(aligned(h * 256 + (1 - half[h]) * 128, 128), 128)

    def own_blocks(n):
        for h in range(2):
            r1[n][h, 0] = st[n, :, c, kept(h), :]
            r1[n][h, 4] = jnp.zeros((2, 128, 128), BF16)

    started = []

    mid = (zl // 2 + zl) % 2

    def home_rows(home):
        return pl.ds(aligned((home - 1) * 32, 32), 32)

    def remote(src, dst, send_sem, recv_sem, to):
        return pltpu.make_async_remote_copy(
            src_ref=src,
            dst_ref=dst,
            send_sem=send_sem,
            recv_sem=recv_sem,
            device_id=to,
            device_id_type=MESH,
        )

    def send(src, dst, send_sem, recv_sem, to):
        cp = remote(src, dst, send_sem, recv_sem, to)
        cp.start()
        started.append(cp)
        return cp

    got = []

    def arrive(cps):
        for cp in cps:
            cp.wait_recv()
            got.append(cp)

    pl.semaphore_wait(barrier, len(partners))

    def to_other_core(n):
        out = []
        for cp in strips[n]:
            cp.wait()
        for h in range(2):
            out.append(
                send(
                    st.at[n, :, oc, given(h), :],
                    so.at[n, h],
                    s0_send.at[n, h],
                    s0_recv.at[n, h],
                    device(x, zh, zl, y, oc),
                )
            )
        return out

    def stage1(n):
        out = []
        for h in range(2):
            out.append(
                send(
                    st.at[n, :, c, given(h), :],
                    r1[n].at[h, 2],
                    s1_send.at[n, h, 0],
                    s1_recv.at[n, h, 0],
                    device(x, zh, zl, first_partner[h], c),
                )
            )
        return out

    def stage1_rest(n, cps):
        out = []
        arrive(cps)
        for h in range(2):
            out.append(
                send(
                    so.at[n, h],
                    r1[n].at[h, 3],
                    s1_send.at[n, h, 1],
                    s1_recv.at[n, h, 1],
                    device(x, zh, zl, first_partner[h], c),
                )
            )
        for h in range(2):
            out.append(
                send(
                    st.at[n, :, oc, kept(h), :],
                    r1[n].at[h, 1],
                    s1_send.at[n, h, 2],
                    s1_recv.at[n, h, 2],
                    device(x, zh, zl, y, oc),
                )
            )
        return out

    def stage2(n, cps):
        out = []
        arrive(cps)
        for h in range(2):
            rows = pl.ds(aligned((1 - quarter[h]) * 64, 64), 64)
            for k in range(2):
                s2[n, h, 2 * k : 2 * k + 2] = r1[n][h, picks[h][k], :, rows, :]
            out.append(
                send(
                    s2.at[n, h],
                    r2.at[n, h],
                    s2_send.at[n, h],
                    s2_recv.at[n, h],
                    device(x, zh, zl, second_partner[h], c),
                )
            )
        return out

    def stage3(n, cps):
        arrive(cps)
        for h in range(2):
            rows = pl.ds(aligned(quarter[h] * 64, 64), 64)
            for k in range(2):
                m2[n, h, 2 * k : 2 * k + 2] = (
                    r1[n][h, picks[h][k], :, rows, :] + r2[n, h, 2 * k : 2 * k + 2]
                )
        a_home, b_home = 1 + zl % 2, 2 - zl % 2
        send(
            m2.at[n, :, :, home_rows(a_home), :],
            r3.at[n, mid],
            s3_send.at[n, 0],
            s3_recv.at[n, mid],
            device(x, zh, a_home, y, c),
        )

        @pl.when(mid == 0)
        def _():
            remote(
                m2.at[n, :, :, home_rows(b_home), :],
                r3.at[n, 2],
                s3_send.at[n, 1],
                s3_recv.at[n, 2],
                device(x, zh, b_home, y, c),
            ).start()

    def spread(n, a, b):
        return remote(
            m3.at[n, :, flip(x, a)],
            r4.at[n, x, :, home_rows(zl), :],
            s4_send.at[n, a, b],
            s4_recv.at[n, a, zl - 1],
            device(flip(x, a), zh, flip(zl, b), y, c),
        )

    def stage4(n):
        @pl.when(mid == 1)
        def _():
            for slot in range(3):
                remote(
                    r3.at[n, slot],
                    r3.at[n, slot],
                    s3_send.at[n, 0],
                    s3_recv.at[n, slot],
                    device(x, zh, zl, y, oc),
                ).wait_recv()
            m3[n] = (
                m2[n, :, :, home_rows(zl), :] + r3[n, 0] + r3[n, 1] + r3[n, 2]
            )
            for b in (1, 2, 3, 0):
                for a in range(4):
                    if a or b:
                        spread(n, a, b).start()
            r4[n, x, :, home_rows(zl), :] = m3[n, :, x]

    def from_home(n, a, home):
        rows = home_rows(home)
        remote(
            r4.at[n, flip(x, a), :, rows, :],
            r4.at[n, flip(x, a), :, rows, :],
            s4_send.at[n, 0, 0],
            s4_recv.at[n, a, home - 1],
            device(x, zh, zl, y, oc),
        ).wait_recv()

    def stage5(n):
        from_home(n, 0, 1 + mid * (2 - zl))
        for a in range(1, 4):
            for home in (1, 2):
                from_home(n, a, home)

        @pl.when(mid == 0)
        def _():
            from_home(n, 0, 2)

        out = []
        for h in range(2):
            rows = pl.ds(aligned(h * 256 + half[h] * 128 + quarter[h] * 64, 64), 64)
            out.append(
                send(
                    r4.at[n, :, h],
                    bmat.at[n, :, rows, :],
                    s5_send.at[n, h],
                    s5_recv.at[n, h],
                    device(x, zh, zl, second_partner[h], c),
                )
            )
            bmat[n, :, rows, :] = r4[n, :, h]
        return out

    def stage6(n, cps):
        out = []
        arrive(cps)
        for h in range(2):
            rows = pl.ds(aligned(h * 256 + half[h] * 128, 128), 128)
            out.append(
                send(
                    bmat.at[n, :, rows, :],
                    bmat.at[n, :, rows, :],
                    s6_send.at[n, h],
                    s6_recv.at[n, h],
                    device(x, zh, zl, first_partner[h], c),
                )
            )
        return out

    def product(n, rows):
        total = jnp.dot(hf[4, rows, :], bmat[n, x], preferred_element_type=F32)
        for at in range(4):
            total = total + jnp.dot(
                hf[at, rows, :], bmat[n, at], preferred_element_type=F32
            )
        return total

    a0 = to_other_core(0)
    a1 = stage1(0)
    a1 += stage1_rest(0, a0)
    own_blocks(0)
    for cp in scalar_loads:
        cp.wait()
    picks = []
    for h in range(2):
        row = []
        for k in range(2):
            o = owner_ref[0, k]
            pick = jnp.int32(4)
            sources = (
                zl * 8 + y * 2 + c,
                zl * 8 + y * 2 + oc,
                zl * 8 + first_partner[h] * 2 + c,
                zl * 8 + first_partner[h] * 2 + oc,
            )
            for at, source in enumerate(sources):
                pick = jnp.where(o == source, at, pick)
            row.append(pick)
        picks.append(row)

    place_rows()
    apply_inverse()
    a2 = stage2(0, a1)
    b0 = to_other_core(1)
    b1 = stage1(1)
    b1 += stage1_rest(1, b0)
    own_blocks(1)
    fold_tiles()
    stage3(0, a2)
    nb_cps = [
        send(band.at[0:64], nb.at[1], nb_send.at[0], nb_recv.at[0], (sub, before)),
        send(band.at[192:256], nb.at[0], nb_send.at[1], nb_recv.at[1], (sub, after)),
    ]
    b2 = stage2(1, b1)
    stage4(0)
    stage3(1, b2)
    arrive(nb_cps)
    for k in range(2):
        at = slice(k * 512, (k + 1) * 512)
        for part in range(2):
            rows = slice(part * 64, (part + 1) * 64)
            full = band[64 + part * 64 : 128 + part * 64, at] + nb[part, :, at]
            high = full.astype(BF16)
            hs[k, rows] = high
            low[k, rows] = (full - high.astype(F32)).astype(BF16)
    own_rows = pl.ds(aligned(c * 128, 128), 128)
    h_cps = []
    for a in range(1, 4):
        h_cps.append(
            send(
                hs.at[flip(x, a) // 2],
                hf.at[x, own_rows, :],
                h_send.at[a],
                h_recv.at[a],
                device(flip(x, a), zh, zl, y, c),
            )
        )
    hf[x, own_rows, :] = hs[x // 2]
    hf[4, own_rows, :] = low[x // 2]

    stage4(1)
    a5 = stage5(0)
    a6 = stage6(0, a5)
    arrive(h_cps)
    h_cps = [
        send(
            hf.at[:, own_rows, :],
            hf.at[:, own_rows, :],
            h_send.at[0],
            h_recv.at[0],
            device(x, zh, zl, y, oc),
        )
    ]
    b5 = stage5(1)
    arrive(h_cps)
    arrive(a6)
    away[...] = product(0, slice(0, 256)).astype(BF16)
    late_cps = [
        send(away, late, late_send.at[0], late_recv.at[0], device(x, 1 - zh, zl, y, c))
    ]
    b6 = stage6(1, b5)
    arrive(b6)
    own = pl.ds(aligned(c * 128, 128), 128)
    other = pl.ds(aligned(oc * 128, 128), 128)
    both = product(1, slice(0, 256))
    pmat[...] = both
    arrive(late_cps)
    away_sum[...] = pmat[other, :] + late[other, :].astype(F32)
    late_cps = [
        send(
            away_sum, cross, late_send.at[1], late_recv.at[1], device(x, zh, zl, y, oc)
        )
    ]
    iface_load.wait()
    out_ref[:, own] = iface[:, own] - (pmat[own, :] + late[own, :].astype(F32))
    arrive(late_cps)
    out_ref[:, other] = iface[:, other] - cross[...]
    for cp in started:
        cp.wait_send()
    for n in range(2):

        @pl.when(mid == 0)
        def _():
            remote(
                m2.at[n, :, :, home_rows(1), :],
                r3.at[n, 2],
                s3_send.at[n, 1],
                s3_recv.at[n, 2],
                device(x, zh, zl, y, oc),
            ).wait_send()

        @pl.when(mid == 1)
        def _():
            for a in range(4):
                for b in range(4):
                    if a or b:
                        spread(n, a, b).wait_send()


def per_device(
    stretch_store,
    stretch_owner,
    tile_map,
    inverse_block,
    face_coupling,
    row_offset,
    row_count,
    interface_block,
):
    hbm = pl.BlockSpec(memory_space=pltpu.HBM)
    dma = pltpu.SemaphoreType.DMA
    return pl.pallas_call(
        kernel,
        out_shape=pltpu.VMEM((128, 256), F32),
        in_specs=[hbm] * 8,
        out_specs=pl.BlockSpec(memory_space=pltpu.VMEM),
        scratch_shapes=[
            pltpu.SMEM((1, 2), jnp.int32),
            pltpu.SMEM((1, 2, 2, 8), jnp.int32),
            pltpu.SMEM((1, 2), jnp.int32),
            pltpu.SMEM((1, 2), jnp.int32),
            pltpu.VMEM((2, 2, 2, 512, 128), BF16),
            pltpu.VMEM((2, 1024, 1024), BF16),
            pltpu.VMEM((2, 1024, 128), BF16),
            pltpu.VMEM((128, 256), F32),
            pltpu.VMEM((2, 5, 2, 128, 128), BF16),
            pltpu.VMEM((2, 5, 2, 128, 128), BF16),
            pltpu.VMEM((2, 2, 2, 128, 128), BF16),
            pltpu.VMEM((2, 2, 4, 64, 128), BF16),
            pltpu.VMEM((2, 2, 4, 64, 128), BF16),
            pltpu.VMEM((2, 2, 4, 64, 128), BF16),
            pltpu.VMEM((2, 3, 2, 4, 32, 128), BF16),
            pltpu.VMEM((2, 2, 4, 32, 128), BF16),
            pltpu.VMEM((2, 4, 2, 64, 128), BF16),
            pltpu.VMEM((2, 4, 512, 128), BF16),
            pltpu.VMEM((2, 256, 1024), BF16),
            pltpu.VMEM((2, 256, 1024), F32),
            pltpu.VMEM((256, 1024), F32),
            pltpu.VMEM((2, 64, 1024), F32),
            pltpu.VMEM((2, 128, 512), BF16),
            pltpu.VMEM((2, 128, 512), BF16),
            pltpu.VMEM((5, 256, 512), BF16),
            pltpu.VMEM((256, 128), F32),
            pltpu.VMEM((256, 128), BF16),
            pltpu.VMEM((128, 128), F32),
            pltpu.VMEM((256, 128), BF16),
            pltpu.VMEM((128, 128), F32),
            dma((16,)),
            dma((2, 2)),
            dma((2, 2)),
            dma((2, 2, 3)),
            dma((2, 2, 3)),
            dma((2, 2)),
            dma((2, 2)),
            dma((2, 2)),
            dma((2, 3)),
            dma((2, 4, 4)),
            dma((2, 4, 2)),
            dma((2, 2)),
            dma((2, 2)),
            dma((2, 2)),
            dma((2, 2)),
            dma((2,)),
            dma((2,)),
            dma((4,)),
            dma((4,)),
            dma((3,)),
            dma((3,)),
        ],
        compiler_params=pltpu.CompilerParams(
            collective_id=0, has_side_effects=True, vmem_limit_bytes=40 * 1024 * 1024
        ),
        name="schur",
    )(
        *(
            pltpu.with_memory_space_constraint(operand, pltpu.HBM)
            for operand in (
                stretch_owner,
                tile_map,
                row_offset,
                row_count,
                stretch_store,
                inverse_block,
                face_coupling,
                interface_block,
            )
        )
    )


def solution(mesh):
    return jax.shard_map(
        per_device,
        mesh=mesh,
        in_specs=(
            P("sub", "ifc", None, None),
            P("sub", None),
            P("sub", "ifc", None, None),
            P("sub", "ifc", None, None),
            P("sub", "ifc", None, None),
            P("sub", "ifc"),
            P("sub", "ifc"),
            P("ifc", "sub"),
        ),
        out_specs=P("ifc", "sub"),
        check_vma=False,
    )
```

```python
import jax
import jax.numpy as jnp
from jax import lax
from jax.experimental import pallas as pl
from jax.experimental.pallas import tpu as pltpu
from jax.sharding import PartitionSpec as P

MESH = pl.DeviceIdType.MESH
F32 = jnp.float32
BF16 = jnp.bfloat16
NT_DIMS = (((1,), (1,)), ((), ()))


def aligned(value, unit):
    return pl.multiple_of(value, unit)


def kernel(
    owner_hbm,
    map_hbm,
    offset_hbm,
    count_hbm,
    store_ref,
    inverse_ref,
    face_ref,
    iface_ref,
    out_ref,
    owner_ref,
    map_ref,
    offset_ref,
    count_ref,
    st,
    inv,
    face,
    iface,
    r1_first,
    r1_second,
    so,
    s2,
    r2,
    m2,
    r3,
    m3,
    r4,
    bmat,
    placed,
    gband,
    band,
    nb,
    hs,
    low,
    hf,
    pmat,
    away,
    away_sum,
    late,
    cross,
    load_sem,
    s0_send,
    s0_recv,
    s1_send,
    s1_recv,
    s2_send,
    s2_recv,
    s3_send,
    s3_recv,
    s4_send,
    s4_recv,
    s5_send,
    s5_recv,
    s6_send,
    s6_recv,
    nb_send,
    nb_recv,
    h_send,
    h_recv,
    late_send,
    late_recv,
    ready,
):
    sub = lax.axis_index("sub")
    ifc = lax.axis_index("ifc")
    x, zh = sub // 2, sub % 2
    zl, y, c = ifc // 8, (ifc // 2) % 4, ifc % 2

    def flip(value, mask):
        out = 0
        for bit in (1, 2):
            digit = (value // bit) % 2
            out = out + bit * ((1 - digit) if mask & bit else digit)
        return out

    def device(x_, zh_, zl_, y_, c_):
        return (x_ * 2 + zh_, zl_ * 8 + y_ * 2 + c_)

    oc = 1 - c
    r1 = (r1_first, r1_second)
    first_partner = (flip(y, 1), flip(y, 3))
    second_partner = (flip(y, 3), flip(y, 1))
    y0, y1 = y % 2, y // 2
    half = ((y0 + y1) % 2, y1)
    quarter = (y1, y0)

    partners = [device(x, zh, zl, y, oc)]
    for h in range(2):
        partners.append(device(x, zh, zl, first_partner[h], c))
    for a in range(4):
        for b in range(4):
            if a or b:
                partners.append(device(flip(x, a), zh, flip(zl, b), y, c))
    before, after = lax.rem(ifc + 31, 32), lax.rem(ifc + 1, 32)
    partners.append((sub, before))
    partners.append((sub, after))
    steps = ((1 - zh), zh)
    strips = ([], [])

    def load_strips(n):
        for xh in range(2):
            for cc in range(2):
                at = aligned(xh * 512 + steps[n] * 256 + cc * 128, 128)
                cp = pltpu.make_async_copy(
                    store_ref.at[0, 0, :, pl.ds(at, 128)],
                    st.at[n, xh, cc],
                    load_sem.at[n * 4 + xh * 2 + cc],
                )
                cp.start()
                strips[n].append(cp)

    load_strips(0)
    barrier = pltpu.get_barrier_semaphore()
    for partner in partners:
        pl.semaphore_signal(barrier, inc=1, device_id=partner, device_id_type=MESH)

    load_strips(1)
    scalar_loads = []
    for at, (src, dst) in enumerate(
        (
            (owner_hbm, owner_ref),
            (map_hbm, map_ref),
            (offset_hbm, offset_ref),
            (count_hbm, count_ref),
        )
    ):
        cp = pltpu.make_async_copy(src, dst, load_sem.at[8 + at])
        cp.start()
        scalar_loads.append(cp)
    face_load = pltpu.make_async_copy(face_ref.at[0], face, load_sem.at[12])
    face_load.start()
    inv_loads = []
    for l in range(2):
        cp = pltpu.make_async_copy(inverse_ref.at[0, l], inv.at[l], load_sem.at[13 + l])
        cp.start()
        inv_loads.append(cp)
    iface_load = pltpu.make_async_copy(iface_ref, iface, load_sem.at[15])
    iface_load.start()

    def place_rows():
        face_load.wait()
        row_at = lax.broadcasted_iota(jnp.int32, (256, 128), 0)
        col_at = lax.broadcasted_iota(jnp.int32, (256, 128), 1)
        for l in range(2):
            start = offset_ref[0, l] - (ifc * 128 - 64)
            here = jnp.logical_and(row_at == col_at + start, col_at < count_ref[0, l])
            place = jnp.where(here, 1.0, 0.0).astype(BF16)
            placed[l] = lax.dot_general(
                place, face[l], NT_DIMS, preferred_element_type=F32
            ).astype(BF16)

    def apply_inverse():
        for l in range(2):
            inv_loads[l].wait()

            def columns(i, _):
                at = pl.ds(aligned(i * 256, 256), 256)
                gband[l, :, at] = jnp.dot(
                    placed[l], inv[l, :, at], preferred_element_type=F32
                )
                return 0

            lax.fori_loop(0, 4, columns, 0)

    def fold_tiles(first, step):
        def fold(r, _):
            rows = pl.ds(aligned((first + r * step) * 64, 64), 64)
            for k in range(2):
                accs = [jnp.zeros((64, 128), F32) for _ in range(4)]
                for l in range(2):
                    for i in range(8):
                        block = gband[l, rows, i * 128 : (i + 1) * 128]
                        tile = map_ref[0, l, k, i]
                        for t in range(4):
                            accs[t] = accs[t] + jnp.where(tile == t, 1.0, 0.0) * block
                for t in range(4):
                    at = k * 512 + t * 128
                    band[rows, at : at + 128] = accs[t]
            return 0

        lax.fori_loop(0, 2, fold, 0)

    def kept(h):
        return pl.ds(aligned(h * 256 + half[h] * 128, 128), 128)

    def given(h):
        return pl.ds(aligned(h * 256 + (1 - half[h]) * 128, 128), 128)

    def own_blocks(n):
        for h in range(2):
            r1[n][h, 0] = st[n, :, c, kept(h), :]
            r1[n][h, 4] = jnp.zeros((2, 128, 128), BF16)

    started = []

    mid = (zl // 2 + zl) % 2

    def home_rows(home):
        return pl.ds(aligned((home - 1) * 32, 32), 32)

    def remote(src, dst, send_sem, recv_sem, to):
        return pltpu.make_async_remote_copy(
            src_ref=src,
            dst_ref=dst,
            send_sem=send_sem,
            recv_sem=recv_sem,
            device_id=to,
            device_id_type=MESH,
        )

    def send(src, dst, send_sem, recv_sem, to):
        cp = remote(src, dst, send_sem, recv_sem, to)
        cp.start()
        started.append(cp)
        return cp

    got = []

    def arrive(cps):
        for cp in cps:
            cp.wait_recv()
            got.append(cp)

    opposite = device(x, 1 - zh, zl, y, c)
    pl.semaphore_wait(barrier, len(partners) + zh)

    @pl.when(zh == 0)
    def _():
        pl.semaphore_signal(barrier, inc=1, device_id=opposite, device_id_type=MESH)

    @pl.when(zh == 1)
    def _():
        pl.semaphore_signal(ready, inc=1, device_id=opposite, device_id_type=MESH)


    def to_other_core(n):
        out = []
        for cp in strips[n]:
            cp.wait()
        for h in range(2):
            out.append(
                send(
                    st.at[n, :, oc, given(h), :],
                    so.at[n, h],
                    s0_send.at[n, h],
                    s0_recv.at[n, h],
                    device(x, zh, zl, y, oc),
                )
            )
        return out

    def stage1(n):
        out = []
        for h in range(2):
            out.append(
                send(
                    st.at[n, :, c, given(h), :],
                    r1[n].at[h, 2],
                    s1_send.at[n, h, 0],
                    s1_recv.at[n, h, 0],
                    device(x, zh, zl, first_partner[h], c),
                )
            )
        return out

    def stage1_rest(n, cps):
        out = []
        arrive(cps)
        for h in range(2):
            out.append(
                send(
                    so.at[n, h],
                    r1[n].at[h, 3],
                    s1_send.at[n, h, 1],
                    s1_recv.at[n, h, 1],
                    device(x, zh, zl, first_partner[h], c),
                )
            )
        for h in range(2):
            out.append(
                send(
                    st.at[n, :, oc, kept(h), :],
                    r1[n].at[h, 1],
                    s1_send.at[n, h, 2],
                    s1_recv.at[n, h, 2],
                    device(x, zh, zl, y, oc),
                )
            )
        return out

    def stage2(n, cps):
        out = []
        arrive(cps)
        for h in range(2):
            rows = pl.ds(aligned((1 - quarter[h]) * 64, 64), 64)
            for k in range(2):
                s2[n, h, 2 * k : 2 * k + 2] = r1[n][h, picks[h][k], :, rows, :]
            out.append(
                send(
                    s2.at[n, h],
                    r2.at[n, h],
                    s2_send.at[n, h],
                    s2_recv.at[n, h],
                    device(x, zh, zl, second_partner[h], c),
                )
            )
        return out

    def stage3(n, cps):
        arrive(cps)
        for h in range(2):
            rows = pl.ds(aligned(quarter[h] * 64, 64), 64)
            for k in range(2):
                m2[n, h, 2 * k : 2 * k + 2] = (
                    r1[n][h, picks[h][k], :, rows, :] + r2[n, h, 2 * k : 2 * k + 2]
                )
        a_home, b_home = 1 + zl % 2, 2 - zl % 2
        send(
            m2.at[n, :, :, home_rows(a_home), :],
            r3.at[n, mid],
            s3_send.at[n, 0],
            s3_recv.at[n, mid],
            device(x, zh, a_home, y, c),
        )

        @pl.when(mid == 0)
        def _():
            remote(
                m2.at[n, :, :, home_rows(b_home), :],
                r3.at[n, 2],
                s3_send.at[n, 1],
                s3_recv.at[n, 2],
                device(x, zh, b_home, y, c),
            ).start()

    def spread(n, a, b):
        return remote(
            m3.at[n, :, flip(x, a)],
            r4.at[n, x, :, home_rows(zl), :],
            s4_send.at[n, a, b],
            s4_recv.at[n, a, zl - 1],
            device(flip(x, a), zh, flip(zl, b), y, c),
        )

    def stage4(n):
        @pl.when(mid == 1)
        def _():
            for slot in range(3):
                remote(
                    r3.at[n, slot],
                    r3.at[n, slot],
                    s3_send.at[n, 0],
                    s3_recv.at[n, slot],
                    device(x, zh, zl, y, oc),
                ).wait_recv()
            m3[n] = (
                m2[n, :, :, home_rows(zl), :] + r3[n, 0] + r3[n, 1] + r3[n, 2]
            )
            for b in (1, 2, 3, 0):
                for a in range(4):
                    if a or b:
                        spread(n, a, b).start()
            r4[n, x, :, home_rows(zl), :] = m3[n, :, x]

    def from_home(n, a, home):
        rows = home_rows(home)
        remote(
            r4.at[n, flip(x, a), :, rows, :],
            r4.at[n, flip(x, a), :, rows, :],
            s4_send.at[n, 0, 0],
            s4_recv.at[n, a, home - 1],
            device(x, zh, zl, y, oc),
        ).wait_recv()

    def stage5(n):
        from_home(n, 0, 1 + mid * (2 - zl))
        for a in range(1, 4):
            for home in (1, 2):
                from_home(n, a, home)

        @pl.when(mid == 0)
        def _():
            from_home(n, 0, 2)

        out = []
        for h in range(2):
            rows = pl.ds(aligned(h * 256 + half[h] * 128 + quarter[h] * 64, 64), 64)
            out.append(
                send(
                    r4.at[n, :, h],
                    bmat.at[n, :, rows, :],
                    s5_send.at[n, h],
                    s5_recv.at[n, h],
                    device(x, zh, zl, second_partner[h], c),
                )
            )
            bmat[n, :, rows, :] = r4[n, :, h]
        return out

    def stage6(n, cps):
        out = []
        arrive(cps)
        for h in range(2):
            rows = pl.ds(aligned(h * 256 + half[h] * 128, 128), 128)
            out.append(
                send(
                    bmat.at[n, :, rows, :],
                    bmat.at[n, :, rows, :],
                    s6_send.at[n, h],
                    s6_recv.at[n, h],
                    device(x, zh, zl, first_partner[h], c),
                )
            )
        return out

    def product(n, rows):
        total = jnp.dot(hf[4, rows, :], bmat[n, x], preferred_element_type=F32)
        for at in range(4):
            total = total + jnp.dot(
                hf[at, rows, :], bmat[n, at], preferred_element_type=F32
            )
        return total

    a0 = to_other_core(0)
    a1 = stage1(0)
    a1 += stage1_rest(0, a0)
    own_blocks(0)
    for cp in scalar_loads:
        cp.wait()
    picks = []
    for h in range(2):
        row = []
        for k in range(2):
            o = owner_ref[0, k]
            pick = jnp.int32(4)
            sources = (
                zl * 8 + y * 2 + c,
                zl * 8 + y * 2 + oc,
                zl * 8 + first_partner[h] * 2 + c,
                zl * 8 + first_partner[h] * 2 + oc,
            )
            for at, source in enumerate(sources):
                pick = jnp.where(o == source, at, pick)
            row.append(pick)
        picks.append(row)

    place_rows()
    apply_inverse()
    a2 = stage2(0, a1)
    b0 = to_other_core(1)
    b1 = stage1(1)
    b1 += stage1_rest(1, b0)
    own_blocks(1)
    stage3(0, a2)
    fold_tiles(0, 3)
    fold_tiles(1, 1)
    nb_cps = [
        send(band.at[0:64], nb.at[1], nb_send.at[0], nb_recv.at[0], (sub, before)),
        send(band.at[192:256], nb.at[0], nb_send.at[1], nb_recv.at[1], (sub, after)),
    ]
    b2 = stage2(1, b1)
    stage4(0)
    stage3(1, b2)
    arrive(nb_cps)
    for k in range(2):
        at = slice(k * 512, (k + 1) * 512)
        for part in range(2):
            rows = slice(part * 64, (part + 1) * 64)
            full = band[64 + part * 64 : 128 + part * 64, at] + nb[part, :, at]
            high = full.astype(BF16)
            hs[k, rows] = high
            low[k, rows] = (full - high.astype(F32)).astype(BF16)
    own_rows = pl.ds(aligned(c * 128, 128), 128)
    h_cps = []
    for a in range(1, 4):
        h_cps.append(
            send(
                hs.at[flip(x, a) // 2],
                hf.at[x, own_rows, :],
                h_send.at[a],
                h_recv.at[a],
                device(flip(x, a), zh, zl, y, c),
            )
        )
    hf[x, own_rows, :] = hs[x // 2]
    hf[4, own_rows, :] = low[x // 2]

    a5 = stage5(0)
    stage4(1)
    a6 = stage6(0, a5)
    arrive(h_cps)
    h_cps = [
        send(
            hf.at[:, own_rows, :],
            hf.at[:, own_rows, :],
            h_send.at[0],
            h_recv.at[0],
            device(x, zh, zl, y, oc),
        )
    ]
    b5 = stage5(1)
    arrive(h_cps)
    arrive(a6)
    away[...] = product(0, slice(0, 256)).astype(BF16)

    @pl.when(zh == 0)
    def _():
        pl.semaphore_wait(ready, 1)

    late_cps = [send(away, late, late_send.at[0], late_recv.at[0], opposite)]
    b6 = stage6(1, b5)
    arrive(b6)
    own = pl.ds(aligned(c * 128, 128), 128)
    other = pl.ds(aligned(oc * 128, 128), 128)
    both = product(1, slice(0, 256))
    pmat[...] = both
    arrive(late_cps)
    away_sum[...] = pmat[other, :] + late[other, :].astype(F32)
    late_cps = [
        send(
            away_sum, cross, late_send.at[1], late_recv.at[1], device(x, zh, zl, y, oc)
        )
    ]
    iface_load.wait()
    out_ref[:, own] = iface[:, own] - (pmat[own, :] + late[own, :].astype(F32))
    arrive(late_cps)
    out_ref[:, other] = iface[:, other] - cross[...]
    for cp in started:
        cp.wait_send()
    for n in range(2):

        @pl.when(mid == 0)
        def _():
            remote(
                m2.at[n, :, :, home_rows(1), :],
                r3.at[n, 2],
                s3_send.at[n, 1],
                s3_recv.at[n, 2],
                device(x, zh, zl, y, oc),
            ).wait_send()

        @pl.when(mid == 1)
        def _():
            for a in range(4):
                for b in range(4):
                    if a or b:
                        spread(n, a, b).wait_send()


def per_device(
    stretch_store,
    stretch_owner,
    tile_map,
    inverse_block,
    face_coupling,
    row_offset,
    row_count,
    interface_block,
):
    hbm = pl.BlockSpec(memory_space=pltpu.HBM)
    dma = pltpu.SemaphoreType.DMA
    return pl.pallas_call(
        kernel,
        out_shape=pltpu.VMEM((128, 256), F32),
        in_specs=[hbm] * 8,
        out_specs=pl.BlockSpec(memory_space=pltpu.VMEM),
        scratch_shapes=[
            pltpu.SMEM((1, 2), jnp.int32),
            pltpu.SMEM((1, 2, 2, 8), jnp.int32),
            pltpu.SMEM((1, 2), jnp.int32),
            pltpu.SMEM((1, 2), jnp.int32),
            pltpu.VMEM((2, 2, 2, 512, 128), BF16),
            pltpu.VMEM((2, 1024, 1024), BF16),
            pltpu.VMEM((2, 1024, 128), BF16),
            pltpu.VMEM((128, 256), F32),
            pltpu.VMEM((2, 5, 2, 128, 128), BF16),
            pltpu.VMEM((2, 5, 2, 128, 128), BF16),
            pltpu.VMEM((2, 2, 2, 128, 128), BF16),
            pltpu.VMEM((2, 2, 4, 64, 128), BF16),
            pltpu.VMEM((2, 2, 4, 64, 128), BF16),
            pltpu.VMEM((2, 2, 4, 64, 128), BF16),
            pltpu.VMEM((2, 3, 2, 4, 32, 128), BF16),
            pltpu.VMEM((2, 2, 4, 32, 128), BF16),
            pltpu.VMEM((2, 4, 2, 64, 128), BF16),
            pltpu.VMEM((2, 4, 512, 128), BF16),
            pltpu.VMEM((2, 256, 1024), BF16),
            pltpu.VMEM((2, 256, 1024), F32),
            pltpu.VMEM((256, 1024), F32),
            pltpu.VMEM((2, 64, 1024), F32),
            pltpu.VMEM((2, 128, 512), BF16),
            pltpu.VMEM((2, 128, 512), BF16),
            pltpu.VMEM((5, 256, 512), BF16),
            pltpu.VMEM((256, 128), F32),
            pltpu.VMEM((256, 128), BF16),
            pltpu.VMEM((128, 128), F32),
            pltpu.VMEM((256, 128), BF16),
            pltpu.VMEM((128, 128), F32),
            dma((16,)),
            dma((2, 2)),
            dma((2, 2)),
            dma((2, 2, 3)),
            dma((2, 2, 3)),
            dma((2, 2)),
            dma((2, 2)),
            dma((2, 2)),
            dma((2, 3)),
            dma((2, 4, 4)),
            dma((2, 4, 2)),
            dma((2, 2)),
            dma((2, 2)),
            dma((2, 2)),
            dma((2, 2)),
            dma((2,)),
            dma((2,)),
            dma((4,)),
            dma((4,)),
            dma((2,)),
            dma((2,)),
            pltpu.SemaphoreType.REGULAR,
        ],
        compiler_params=pltpu.CompilerParams(
            collective_id=0, has_side_effects=True, vmem_limit_bytes=40 * 1024 * 1024
        ),
        name="schur",
    )(
        *(
            pltpu.with_memory_space_constraint(operand, pltpu.HBM)
            for operand in (
                stretch_owner,
                tile_map,
                row_offset,
                row_count,
                stretch_store,
                inverse_block,
                face_coupling,
                interface_block,
            )
        )
    )


def solution(mesh):
    return jax.shard_map(
        per_device,
        mesh=mesh,
        in_specs=(
            P("sub", "ifc", None, None),
            P("sub", None),
            P("sub", "ifc", None, None),
            P("sub", "ifc", None, None),
            P("sub", "ifc", None, None),
            P("sub", "ifc"),
            P("sub", "ifc"),
            P("ifc", "sub"),
        ),
        out_specs=P("ifc", "sub"),
        check_vma=False,
    )
```

```python
import jax
import jax.numpy as jnp
from jax import lax
from jax.experimental import pallas as pl
from jax.experimental.pallas import tpu as pltpu
from jax.sharding import PartitionSpec as P

MESH = pl.DeviceIdType.MESH
F32 = jnp.float32
BF16 = jnp.bfloat16
NT_DIMS = (((1,), (1,)), ((), ()))


def aligned(value, unit):
    return pl.multiple_of(value, unit)


def kernel(
    owner_hbm,
    map_hbm,
    offset_hbm,
    count_hbm,
    store_ref,
    inverse_ref,
    face_ref,
    iface_ref,
    out_ref,
    owner_ref,
    map_ref,
    offset_ref,
    count_ref,
    st,
    inv,
    face,
    iface,
    r1_first,
    r1_second,
    so,
    s2,
    r2,
    m2,
    r3,
    m3,
    r4,
    bmat,
    placed,
    gband,
    band,
    nb,
    hs,
    low,
    hf,
    pmat,
    away,
    late,
    cross,
    load_sem,
    s0_send,
    s0_recv,
    s1_send,
    s1_recv,
    s2_send,
    s2_recv,
    s3_send,
    s3_recv,
    s4_send,
    s4_recv,
    s5_send,
    s5_recv,
    s6_send,
    s6_recv,
    nb_send,
    nb_recv,
    h_send,
    h_recv,
    late_send,
    late_recv,
    ready,
):
    sub = lax.axis_index("sub")
    ifc = lax.axis_index("ifc")
    x, zh = sub // 2, sub % 2
    zl, y, c = ifc // 8, (ifc // 2) % 4, ifc % 2

    def flip(value, mask):
        out = 0
        for bit in (1, 2):
            digit = (value // bit) % 2
            out = out + bit * ((1 - digit) if mask & bit else digit)
        return out

    def device(x_, zh_, zl_, y_, c_):
        return (x_ * 2 + zh_, zl_ * 8 + y_ * 2 + c_)

    oc = 1 - c
    r1 = (r1_first, r1_second)
    first_partner = (flip(y, 1), flip(y, 3))
    second_partner = (flip(y, 3), flip(y, 1))
    y0, y1 = y % 2, y // 2
    half = ((y0 + y1) % 2, y1)
    quarter = (y1, y0)

    partners = [device(x, zh, zl, y, oc)]
    for h in range(2):
        partners.append(device(x, zh, zl, first_partner[h], c))
    for a in range(4):
        for b in range(3):
            if a or b:
                partners.append(device(flip(x, a), zh, flip(zl, b), y, c))
    before, after = lax.rem(ifc + 31, 32), lax.rem(ifc + 1, 32)
    partners.append((sub, lax.rem(ifc + 31 + 2 * c, 32)))
    mid = (zl // 2 + zl) % 2
    steps = ((1 - zh), zh)
    strips = ([], [])

    def load_strips(n):
        for xh in range(2):
            for cc in range(2):
                at = aligned(xh * 512 + steps[n] * 256 + cc * 128, 128)
                cp = pltpu.make_async_copy(
                    store_ref.at[0, 0, :, pl.ds(at, 128)],
                    st.at[n, xh, cc],
                    load_sem.at[n * 4 + xh * 2 + cc],
                )
                cp.start()
                strips[n].append(cp)

    load_strips(0)
    barrier = pltpu.get_barrier_semaphore()
    for partner in partners:
        pl.semaphore_signal(barrier, inc=1, device_id=partner, device_id_type=MESH)

    @pl.when(mid == 1)
    def _():
        for a in range(4):
            pl.semaphore_signal(
                barrier,
                inc=1,
                device_id=device(flip(x, a), zh, 3 - zl, y, c),
                device_id_type=MESH,
            )


    load_strips(1)
    scalar_loads = []
    for at, (src, dst) in enumerate(
        (
            (owner_hbm, owner_ref),
            (map_hbm, map_ref),
            (offset_hbm, offset_ref),
            (count_hbm, count_ref),
        )
    ):
        cp = pltpu.make_async_copy(src, dst, load_sem.at[8 + at])
        cp.start()
        scalar_loads.append(cp)
    face_load = pltpu.make_async_copy(face_ref.at[0], face, load_sem.at[12])
    face_load.start()
    inv_loads = []
    for l in range(2):
        cp = pltpu.make_async_copy(inverse_ref.at[0, l], inv.at[l], load_sem.at[13 + l])
        cp.start()
        inv_loads.append(cp)
    iface_load = pltpu.make_async_copy(iface_ref, iface, load_sem.at[15])
    iface_load.start()

    def place_rows():
        face_load.wait()
        row_at = lax.broadcasted_iota(jnp.int32, (256, 128), 0)
        col_at = lax.broadcasted_iota(jnp.int32, (256, 128), 1)
        for l in range(2):
            start = offset_ref[0, l] - (ifc * 128 - 64)
            here = jnp.logical_and(row_at == col_at + start, col_at < count_ref[0, l])
            place = jnp.where(here, 1.0, 0.0).astype(BF16)
            placed[l] = lax.dot_general(
                place, face[l], NT_DIMS, preferred_element_type=F32
            ).astype(BF16)

    def apply_inverse():
        for l in range(2):
            inv_loads[l].wait()

            def columns(i, _):
                at = pl.ds(aligned(i * 256, 256), 256)
                gband[l, :, at] = jnp.dot(
                    placed[l], inv[l, :, at], preferred_element_type=F32
                )
                return 0

            lax.fori_loop(0, 4, columns, 0)

    def fold_tiles(first, step):
        def fold(r, _):
            rows = pl.ds(aligned((first + r * step) * 64, 64), 64)
            for k in range(2):
                accs = [jnp.zeros((64, 128), F32) for _ in range(4)]
                for l in range(2):
                    for i in range(8):
                        block = gband[l, rows, i * 128 : (i + 1) * 128]
                        tile = map_ref[0, l, k, i]
                        for t in range(4):
                            accs[t] = accs[t] + jnp.where(tile == t, 1.0, 0.0) * block
                for t in range(4):
                    at = k * 512 + t * 128
                    band[rows, at : at + 128] = accs[t]
            return 0

        lax.fori_loop(0, 2, fold, 0)

    def kept(h):
        return pl.ds(aligned(h * 256 + half[h] * 128, 128), 128)

    def given(h):
        return pl.ds(aligned(h * 256 + (1 - half[h]) * 128, 128), 128)

    def own_blocks(n):
        for h in range(2):
            r1[n][h, 0] = st[n, :, c, kept(h), :]
            r1[n][h, 4] = jnp.zeros((2, 128, 128), BF16)

    started = []

    def home_rows(home):
        return pl.ds(aligned((home - 1) * 32, 32), 32)

    def remote(src, dst, send_sem, recv_sem, to):
        return pltpu.make_async_remote_copy(
            src_ref=src,
            dst_ref=dst,
            send_sem=send_sem,
            recv_sem=recv_sem,
            device_id=to,
            device_id_type=MESH,
        )

    def send(src, dst, send_sem, recv_sem, to):
        cp = remote(src, dst, send_sem, recv_sem, to)
        cp.start()
        started.append(cp)
        return cp

    got = []

    def arrive(cps):
        for cp in cps:
            cp.wait_recv()
            got.append(cp)

    opposite = device(x, 1 - zh, zl, y, c)
    pl.semaphore_wait(barrier, len(partners) + 2 * zh + 4 * mid)

    opposites = (opposite, device(x, 1 - zh, zl, y, oc))

    @pl.when(zh == 0)
    def _():
        for to in opposites:
            pl.semaphore_signal(barrier, inc=1, device_id=to, device_id_type=MESH)

    @pl.when(zh == 1)
    def _():
        for to in opposites:
            pl.semaphore_signal(ready, inc=1, device_id=to, device_id_type=MESH)


    def to_other_core(n):
        out = []
        for h in range(2):
            out.append(
                send(
                    st.at[n, :, oc, given(h), :],
                    so.at[n, h],
                    s0_send.at[n, h],
                    s0_recv.at[n, h],
                    device(x, zh, zl, y, oc),
                )
            )
        return out

    def stage1(n):
        out = []
        for cp in strips[n]:
            cp.wait()
        for h in range(2):
            out.append(
                send(
                    st.at[n, :, c, given(h), :],
                    r1[n].at[h, 2],
                    s1_send.at[n, h, 0],
                    s1_recv.at[n, h, 0],
                    device(x, zh, zl, first_partner[h], c),
                )
            )
        return out

    def stage1_rest(n, cps):
        out = []
        arrive(cps)
        for h in range(2):
            out.append(
                send(
                    so.at[n, h],
                    r1[n].at[h, 3],
                    s1_send.at[n, h, 1],
                    s1_recv.at[n, h, 1],
                    device(x, zh, zl, first_partner[h], c),
                )
            )
        for h in range(2):
            out.append(
                send(
                    st.at[n, :, oc, kept(h), :],
                    r1[n].at[h, 1],
                    s1_send.at[n, h, 2],
                    s1_recv.at[n, h, 2],
                    device(x, zh, zl, y, oc),
                )
            )
        return out

    def stage2(n, cps):
        out = []
        arrive(cps)
        for h in range(2):
            rows = pl.ds(aligned((1 - quarter[h]) * 64, 64), 64)
            for k in range(2):
                s2[n, h, 2 * k : 2 * k + 2] = r1[n][h, picks[h][k], :, rows, :]
            out.append(
                send(
                    s2.at[n, h],
                    r2.at[n, h],
                    s2_send.at[n, h],
                    s2_recv.at[n, h],
                    device(x, zh, zl, second_partner[h], c),
                )
            )
        return out

    def stage3(n, cps):
        arrive(cps)
        for h in range(2):
            rows = pl.ds(aligned(quarter[h] * 64, 64), 64)
            for k in range(2):
                m2[n, h, 2 * k : 2 * k + 2] = (
                    r1[n][h, picks[h][k], :, rows, :] + r2[n, h, 2 * k : 2 * k + 2]
                )
        a_home, b_home = 1 + zl % 2, 2 - zl % 2
        send(
            m2.at[n, :, :, home_rows(a_home), :],
            r3.at[n, mid],
            s3_send.at[n, 0],
            s3_recv.at[n, mid],
            device(x, zh, a_home, y, c),
        )

        @pl.when(mid == 0)
        def _():
            remote(
                m2.at[n, :, :, home_rows(b_home), :],
                r3.at[n, 2],
                s3_send.at[n, 1],
                s3_recv.at[n, 2],
                device(x, zh, b_home, y, c),
            ).start()

    def spread(n, a, b):
        return remote(
            m3.at[n, :, flip(x, a)],
            r4.at[n, x, :, home_rows(zl), :],
            s4_send.at[n, a, b],
            s4_recv.at[n, a, zl - 1],
            device(flip(x, a), zh, flip(zl, b), y, c),
        )

    def stage4(n):
        @pl.when(mid == 1)
        def _():
            for slot in range(3):
                remote(
                    r3.at[n, slot],
                    r3.at[n, slot],
                    s3_send.at[n, 0],
                    s3_recv.at[n, slot],
                    device(x, zh, zl, y, oc),
                ).wait_recv()
            m3[n] = (
                m2[n, :, :, home_rows(zl), :] + r3[n, 0] + r3[n, 1] + r3[n, 2]
            )
            for b in (2, 3, 1, 0):
                for a in (2, 1, 3, 0):
                    if a or b:
                        spread(n, a, b).start()
            r4[n, x, :, home_rows(zl), :] = m3[n, :, x]

    def from_home(n, a, home):
        rows = home_rows(home)
        remote(
            r4.at[n, flip(x, a), :, rows, :],
            r4.at[n, flip(x, a), :, rows, :],
            s4_send.at[n, 0, 0],
            s4_recv.at[n, a, home - 1],
            device(x, zh, zl, y, oc),
        ).wait_recv()

    def stage5(n):
        from_home(n, 0, 1 + mid * (2 - zl))
        for a in range(1, 4):
            for home in (1, 2):
                from_home(n, a, home)

        @pl.when(mid == 0)
        def _():
            from_home(n, 0, 2)

        out = []
        for h in range(2):
            rows = pl.ds(aligned(h * 256 + half[h] * 128 + quarter[h] * 64, 64), 64)
            out.append(
                send(
                    r4.at[n, :, h],
                    bmat.at[n, :, rows, :],
                    s5_send.at[n, h],
                    s5_recv.at[n, h],
                    device(x, zh, zl, second_partner[h], c),
                )
            )
            bmat[n, :, rows, :] = r4[n, :, h]
        return out

    def stage6(n, cps):
        out = []
        arrive(cps)
        for h in range(2):
            rows = pl.ds(aligned(h * 256 + half[h] * 128, 128), 128)
            out.append(
                send(
                    bmat.at[n, :, rows, :],
                    bmat.at[n, :, rows, :],
                    s6_send.at[n, h],
                    s6_recv.at[n, h],
                    device(x, zh, zl, first_partner[h], c),
                )
            )
        return out

    def product(n, rows):
        total = jnp.dot(hf[4, rows, :], bmat[n, x], preferred_element_type=F32)
        for at in range(4):
            total = total + jnp.dot(
                hf[at, rows, :], bmat[n, at], preferred_element_type=F32
            )
        return total

    a1 = stage1(0)
    a0 = to_other_core(0)
    a1 += stage1_rest(0, a0)
    own_blocks(0)
    for cp in scalar_loads:
        cp.wait()
    picks = []
    for h in range(2):
        row = []
        for k in range(2):
            o = owner_ref[0, k]
            pick = jnp.int32(4)
            sources = (
                zl * 8 + y * 2 + c,
                zl * 8 + y * 2 + oc,
                zl * 8 + first_partner[h] * 2 + c,
                zl * 8 + first_partner[h] * 2 + oc,
            )
            for at, source in enumerate(sources):
                pick = jnp.where(o == source, at, pick)
            row.append(pick)
        picks.append(row)

    place_rows()
    apply_inverse()
    a2 = stage2(0, a1)
    b1 = stage1(1)
    b0 = to_other_core(1)
    b1 += stage1_rest(1, b0)
    own_blocks(1)
    stage3(0, a2)
    fold_tiles(0, 3)
    fold_tiles(1, 1)
    nb_cps = [
        send(band.at[0:64], nb.at[1], nb_send.at[0], nb_recv.at[0], (sub, before)),
        send(band.at[192:256], nb.at[0], nb_send.at[1], nb_recv.at[1], (sub, after)),
    ]
    b2 = stage2(1, b1)
    stage4(0)
    stage3(1, b2)
    arrive(nb_cps)
    for k in range(2):
        at = slice(k * 512, (k + 1) * 512)
        for part in range(2):
            rows = slice(part * 64, (part + 1) * 64)
            full = band[64 + part * 64 : 128 + part * 64, at] + nb[part, :, at]
            high = full.astype(BF16)
            hs[k, rows] = high
            low[k, rows] = (full - high.astype(F32)).astype(BF16)
    own_rows = pl.ds(aligned(c * 128, 128), 128)
    h_cps = []
    for a in range(1, 4):
        h_cps.append(
            send(
                hs.at[flip(x, a) // 2],
                hf.at[x, own_rows, :],
                h_send.at[a],
                h_recv.at[a],
                device(flip(x, a), zh, zl, y, c),
            )
        )
    hf[x, own_rows, :] = hs[x // 2]
    hf[4, own_rows, :] = low[x // 2]

    a5 = stage5(0)
    stage4(1)
    a6 = stage6(0, a5)
    arrive(h_cps)
    h_cps = [
        send(
            hf.at[:, own_rows, :],
            hf.at[:, own_rows, :],
            h_send.at[0],
            h_recv.at[0],
            device(x, zh, zl, y, oc),
        )
    ]
    b5 = stage5(1)
    arrive(h_cps)
    arrive(a6)
    @pl.when(zh == 0)
    def _():
        pl.semaphore_wait(ready, 2)

    late_cps = []
    for d, core in enumerate((c, oc)):
        rows = pl.ds(aligned(core * 128, 128), 128)
        away[d] = product(0, rows).astype(BF16)
        late_cps.append(
            send(away.at[d], late.at[d], late_send.at[d], late_recv.at[d], opposites[d])
        )
    b6 = stage6(1, b5)
    arrive(b6)
    own = pl.ds(aligned(c * 128, 128), 128)
    other = pl.ds(aligned(oc * 128, 128), 128)
    pmat[...] = product(1, other)
    late_cps.append(
        send(pmat, cross, late_send.at[2], late_recv.at[2], device(x, zh, zl, y, oc))
    )
    mine = product(1, own)
    iface_load.wait()
    out_ref[:, own] = iface[:, own] - mine
    arrive(late_cps)
    out_ref[:, own] = out_ref[:, own] - late[0].astype(F32)
    out_ref[:, other] = iface[:, other] - (cross[...] + late[1].astype(F32))
    for cp in started:
        cp.wait_send()
    for n in range(2):

        @pl.when(mid == 0)
        def _():
            remote(
                m2.at[n, :, :, home_rows(1), :],
                r3.at[n, 2],
                s3_send.at[n, 1],
                s3_recv.at[n, 2],
                device(x, zh, zl, y, oc),
            ).wait_send()

        @pl.when(mid == 1)
        def _():
            for a in range(4):
                for b in range(4):
                    if a or b:
                        spread(n, a, b).wait_send()


def per_device(
    stretch_store,
    stretch_owner,
    tile_map,
    inverse_block,
    face_coupling,
    row_offset,
    row_count,
    interface_block,
):
    hbm = pl.BlockSpec(memory_space=pltpu.HBM)
    dma = pltpu.SemaphoreType.DMA
    return pl.pallas_call(
        kernel,
        out_shape=pltpu.VMEM((128, 256), F32),
        in_specs=[hbm] * 8,
        out_specs=pl.BlockSpec(memory_space=pltpu.VMEM),
        scratch_shapes=[
            pltpu.SMEM((1, 2), jnp.int32),
            pltpu.SMEM((1, 2, 2, 8), jnp.int32),
            pltpu.SMEM((1, 2), jnp.int32),
            pltpu.SMEM((1, 2), jnp.int32),
            pltpu.VMEM((2, 2, 2, 512, 128), BF16),
            pltpu.VMEM((2, 1024, 1024), BF16),
            pltpu.VMEM((2, 1024, 128), BF16),
            pltpu.VMEM((128, 256), F32),
            pltpu.VMEM((2, 5, 2, 128, 128), BF16),
            pltpu.VMEM((2, 5, 2, 128, 128), BF16),
            pltpu.VMEM((2, 2, 2, 128, 128), BF16),
            pltpu.VMEM((2, 2, 4, 64, 128), BF16),
            pltpu.VMEM((2, 2, 4, 64, 128), BF16),
            pltpu.VMEM((2, 2, 4, 64, 128), BF16),
            pltpu.VMEM((2, 3, 2, 4, 32, 128), BF16),
            pltpu.VMEM((2, 2, 4, 32, 128), BF16),
            pltpu.VMEM((2, 4, 2, 64, 128), BF16),
            pltpu.VMEM((2, 4, 512, 128), BF16),
            pltpu.VMEM((2, 256, 1024), BF16),
            pltpu.VMEM((2, 256, 1024), F32),
            pltpu.VMEM((256, 1024), F32),
            pltpu.VMEM((2, 64, 1024), F32),
            pltpu.VMEM((2, 128, 512), BF16),
            pltpu.VMEM((2, 128, 512), BF16),
            pltpu.VMEM((5, 256, 512), BF16),
            pltpu.VMEM((128, 128), F32),
            pltpu.VMEM((2, 128, 128), BF16),
            pltpu.VMEM((2, 128, 128), BF16),
            pltpu.VMEM((128, 128), F32),
            dma((16,)),
            dma((2, 2)),
            dma((2, 2)),
            dma((2, 2, 3)),
            dma((2, 2, 3)),
            dma((2, 2)),
            dma((2, 2)),
            dma((2, 2)),
            dma((2, 3)),
            dma((2, 4, 4)),
            dma((2, 4, 2)),
            dma((2, 2)),
            dma((2, 2)),
            dma((2, 2)),
            dma((2, 2)),
            dma((2,)),
            dma((2,)),
            dma((4,)),
            dma((4,)),
            dma((3,)),
            dma((3,)),
            pltpu.SemaphoreType.REGULAR,
        ],
        compiler_params=pltpu.CompilerParams(
            collective_id=0, has_side_effects=True, vmem_limit_bytes=40 * 1024 * 1024
        ),
        name="schur",
    )(
        *(
            pltpu.with_memory_space_constraint(operand, pltpu.HBM)
            for operand in (
                stretch_owner,
                tile_map,
                row_offset,
                row_count,
                stretch_store,
                inverse_block,
                face_coupling,
                interface_block,
            )
        )
    )


def solution(mesh):
    return jax.shard_map(
        per_device,
        mesh=mesh,
        in_specs=(
            P("sub", "ifc", None, None),
            P("sub", None),
            P("sub", "ifc", None, None),
            P("sub", "ifc", None, None),
            P("sub", "ifc", None, None),
            P("sub", "ifc"),
            P("sub", "ifc"),
            P("ifc", "sub"),
        ),
        out_specs=P("ifc", "sub"),
        check_vma=False,
    )
```

```python
import jax
import jax.numpy as jnp
from jax import lax
from jax.experimental import pallas as pl
from jax.experimental.pallas import tpu as pltpu
from jax.sharding import PartitionSpec as P

MESH = pl.DeviceIdType.MESH
F32 = jnp.float32
BF16 = jnp.bfloat16
NT_DIMS = (((1,), (1,)), ((), ()))


def aligned(value, unit):
    return pl.multiple_of(value, unit)


def kernel(
    owner_hbm,
    map_hbm,
    offset_hbm,
    count_hbm,
    store_ref,
    inverse_ref,
    face_ref,
    iface_ref,
    out_ref,
    owner_ref,
    map_ref,
    offset_ref,
    count_ref,
    st,
    inv,
    face,
    iface,
    r1_first,
    r1_second,
    so,
    s2,
    r2,
    m2,
    r3,
    m3,
    r4,
    bmat,
    placed,
    gband,
    band,
    nb,
    hs,
    low,
    hf,
    pmat,
    away,
    late,
    cross,
    load_sem,
    s0_send,
    s0_recv,
    s1_send,
    s1_recv,
    s2_send,
    s2_recv,
    s3_send,
    s3_recv,
    s4_send,
    s4_recv,
    s5_send,
    s5_recv,
    s6_send,
    s6_recv,
    nb_send,
    nb_recv,
    h_send,
    h_recv,
    late_send,
    late_recv,
    ready,
):
    sub = lax.axis_index("sub")
    ifc = lax.axis_index("ifc")
    x, zh = sub // 2, sub % 2
    zl, y, c = ifc // 8, (ifc // 2) % 4, ifc % 2

    def flip(value, mask):
        out = 0
        for bit in (1, 2):
            digit = (value // bit) % 2
            out = out + bit * ((1 - digit) if mask & bit else digit)
        return out

    def device(x_, zh_, zl_, y_, c_):
        return (x_ * 2 + zh_, zl_ * 8 + y_ * 2 + c_)

    oc = 1 - c
    r1 = (r1_first, r1_second)
    first_partner = (flip(y, 1), flip(y, 3))
    second_partner = (flip(y, 3), flip(y, 1))
    y0, y1 = y % 2, y // 2
    half = ((y0 + y1) % 2, y1)
    quarter = (y1, y0)

    partners = [device(x, zh, zl, y, oc)]
    for h in range(2):
        partners.append(device(x, zh, zl, first_partner[h], c))
    for a in range(4):
        for b in range(3):
            if a or b:
                partners.append(device(flip(x, a), zh, flip(zl, b), y, c))
    before, after = lax.rem(ifc + 31, 32), lax.rem(ifc + 1, 32)
    partners.append((sub, lax.rem(ifc + 31 + 2 * c, 32)))
    mid = (zl // 2 + zl) % 2
    steps = ((1 - zh), zh)
    strips = ([], [])

    def load_strips(n):
        for xh in range(2):
            for cc in range(2):
                at = aligned(xh * 512 + steps[n] * 256 + cc * 128, 128)
                cp = pltpu.make_async_copy(
                    store_ref.at[0, 0, :, pl.ds(at, 128)],
                    st.at[n, xh, cc],
                    load_sem.at[n * 4 + xh * 2 + cc],
                )
                cp.start()
                strips[n].append(cp)

    load_strips(0)
    barrier = pltpu.get_barrier_semaphore()
    for partner in partners:
        pl.semaphore_signal(barrier, inc=1, device_id=partner, device_id_type=MESH)

    @pl.when(mid == 1)
    def _():
        for a in range(4):
            pl.semaphore_signal(
                barrier,
                inc=1,
                device_id=device(flip(x, a), zh, 3 - zl, y, c),
                device_id_type=MESH,
            )


    load_strips(1)
    scalar_loads = []
    for at, (src, dst) in enumerate(
        (
            (owner_hbm, owner_ref),
            (map_hbm, map_ref),
            (offset_hbm, offset_ref),
            (count_hbm, count_ref),
        )
    ):
        cp = pltpu.make_async_copy(src, dst, load_sem.at[8 + at])
        cp.start()
        scalar_loads.append(cp)
    face_load = pltpu.make_async_copy(face_ref.at[0], face, load_sem.at[12])
    face_load.start()
    inv_loads = []
    for l in range(2):
        cp = pltpu.make_async_copy(inverse_ref.at[0, l], inv.at[l], load_sem.at[13 + l])
        cp.start()
        inv_loads.append(cp)
    iface_load = pltpu.make_async_copy(iface_ref, iface, load_sem.at[15])
    iface_load.start()

    def place_rows():
        face_load.wait()
        row_at = lax.broadcasted_iota(jnp.int32, (256, 128), 0)
        col_at = lax.broadcasted_iota(jnp.int32, (256, 128), 1)
        for l in range(2):
            start = offset_ref[0, l] - (ifc * 128 - 64)
            here = jnp.logical_and(row_at == col_at + start, col_at < count_ref[0, l])
            place = jnp.where(here, 1.0, 0.0).astype(BF16)
            placed[l] = lax.dot_general(
                place, face[l], NT_DIMS, preferred_element_type=F32
            ).astype(BF16)

    def apply_inverse():
        for l in range(2):
            inv_loads[l].wait()

            def columns(i, _):
                at = pl.ds(aligned(i * 256, 256), 256)
                gband[l, :, at] = jnp.dot(
                    placed[l], inv[l, :, at], preferred_element_type=F32
                )
                return 0

            lax.fori_loop(0, 4, columns, 0)

    def fold_tiles(first, step):
        def fold(r, _):
            rows = pl.ds(aligned((first + r * step) * 64, 64), 64)
            for k in range(2):
                accs = [jnp.zeros((64, 128), F32) for _ in range(4)]
                for l in range(2):
                    for i in range(8):
                        block = gband[l, rows, i * 128 : (i + 1) * 128]
                        tile = map_ref[0, l, k, i]
                        for t in range(4):
                            accs[t] = accs[t] + jnp.where(tile == t, 1.0, 0.0) * block
                for t in range(4):
                    at = k * 512 + t * 128
                    band[rows, at : at + 128] = accs[t]
            return 0

        lax.fori_loop(0, 2, fold, 0)

    def kept(h):
        return pl.ds(aligned(h * 256 + half[h] * 128, 128), 128)

    def given(h):
        return pl.ds(aligned(h * 256 + (1 - half[h]) * 128, 128), 128)

    def own_blocks(n):
        for h in range(2):
            r1[n][h, 0] = st[n, :, c, kept(h), :]
            r1[n][h, 4] = jnp.zeros((2, 128, 128), BF16)

    started = []

    def home_rows(home):
        return pl.ds(aligned((home - 1) * 32, 32), 32)

    def remote(src, dst, send_sem, recv_sem, to):
        return pltpu.make_async_remote_copy(
            src_ref=src,
            dst_ref=dst,
            send_sem=send_sem,
            recv_sem=recv_sem,
            device_id=to,
            device_id_type=MESH,
        )

    def send(src, dst, send_sem, recv_sem, to):
        cp = remote(src, dst, send_sem, recv_sem, to)
        cp.start()
        started.append(cp)
        return cp

    got = []

    def arrive(cps):
        for cp in cps:
            cp.wait_recv()
            got.append(cp)

    opposite = device(x, 1 - zh, zl, y, c)
    pl.semaphore_wait(barrier, len(partners) + 2 * zh + 4 * mid)

    opposites = (opposite, device(x, 1 - zh, zl, y, oc))

    @pl.when(zh == 0)
    def _():
        for to in opposites:
            pl.semaphore_signal(barrier, inc=1, device_id=to, device_id_type=MESH)

    @pl.when(zh == 1)
    def _():
        for to in opposites:
            pl.semaphore_signal(ready, inc=1, device_id=to, device_id_type=MESH)


    def to_other_core(n):
        out = []
        for h in range(2):
            out.append(
                send(
                    st.at[n, :, oc, given(h), :],
                    so.at[n, h],
                    s0_send.at[n, h],
                    s0_recv.at[n, h],
                    device(x, zh, zl, y, oc),
                )
            )
        return out

    def stage1(n):
        out = []
        for cp in strips[n]:
            cp.wait()
        for h in range(2):
            out.append(
                send(
                    st.at[n, :, c, given(h), :],
                    r1[n].at[h, 2],
                    s1_send.at[n, h, 0],
                    s1_recv.at[n, h, 0],
                    device(x, zh, zl, first_partner[h], c),
                )
            )
        return out

    def stage1_rest(n, cps):
        out = []
        arrive(cps)
        for h in range(2):
            out.append(
                send(
                    so.at[n, h],
                    r1[n].at[h, 3],
                    s1_send.at[n, h, 1],
                    s1_recv.at[n, h, 1],
                    device(x, zh, zl, first_partner[h], c),
                )
            )
        for h in range(2):
            out.append(
                send(
                    st.at[n, :, oc, kept(h), :],
                    r1[n].at[h, 1],
                    s1_send.at[n, h, 2],
                    s1_recv.at[n, h, 2],
                    device(x, zh, zl, y, oc),
                )
            )
        return out

    def stage2(n, cps):
        out = []
        arrive(cps)
        for h in range(2):
            rows = pl.ds(aligned((1 - quarter[h]) * 64, 64), 64)
            for k in range(2):
                s2[n, h, 2 * k : 2 * k + 2] = r1[n][h, picks[h][k], :, rows, :]
            out.append(
                send(
                    s2.at[n, h],
                    r2.at[n, h],
                    s2_send.at[n, h],
                    s2_recv.at[n, h],
                    device(x, zh, zl, second_partner[h], c),
                )
            )
        return out

    def stage3(n, cps):
        arrive(cps)
        for h in range(2):
            rows = pl.ds(aligned(quarter[h] * 64, 64), 64)
            for k in range(2):
                m2[n, h, 2 * k : 2 * k + 2] = (
                    r1[n][h, picks[h][k], :, rows, :] + r2[n, h, 2 * k : 2 * k + 2]
                )
        a_home, b_home = 1 + zl % 2, 2 - zl % 2
        send(
            m2.at[n, :, :, home_rows(a_home), :],
            r3.at[n, mid],
            s3_send.at[n, 0],
            s3_recv.at[n, mid],
            device(x, zh, a_home, y, c),
        )

        @pl.when(mid == 0)
        def _():
            remote(
                m2.at[n, :, :, home_rows(b_home), :],
                r3.at[n, 2],
                s3_send.at[n, 1],
                s3_recv.at[n, 2],
                device(x, zh, b_home, y, c),
            ).start()

    def spread(n, a, b):
        return remote(
            m3.at[n, :, flip(x, a)],
            r4.at[n, x, :, home_rows(zl), :],
            s4_send.at[n, a, b],
            s4_recv.at[n, a, zl - 1],
            device(flip(x, a), zh, flip(zl, b), y, c),
        )

    def stage4(n):
        @pl.when(mid == 1)
        def _():
            for slot in range(3):
                remote(
                    r3.at[n, slot],
                    r3.at[n, slot],
                    s3_send.at[n, 0],
                    s3_recv.at[n, slot],
                    device(x, zh, zl, y, oc),
                ).wait_recv()
            m3[n] = (
                m2[n, :, :, home_rows(zl), :] + r3[n, 0] + r3[n, 1] + r3[n, 2]
            )
            for b in (2, 3, 1, 0):
                for a in (2, 1, 3, 0):
                    if a or b:
                        spread(n, a, b).start()
            r4[n, x, :, home_rows(zl), :] = m3[n, :, x]

    def from_home(n, a, home):
        rows = home_rows(home)
        remote(
            r4.at[n, flip(x, a), :, rows, :],
            r4.at[n, flip(x, a), :, rows, :],
            s4_send.at[n, 0, 0],
            s4_recv.at[n, a, home - 1],
            device(x, zh, zl, y, oc),
        ).wait_recv()

    def stage5(n):
        from_home(n, 0, 1 + mid * (2 - zl))
        for a in range(1, 4):
            for home in (1, 2):
                from_home(n, a, home)

        @pl.when(mid == 0)
        def _():
            from_home(n, 0, 2)

        out = []
        for h in range(2):
            rows = pl.ds(aligned(h * 256 + half[h] * 128 + quarter[h] * 64, 64), 64)
            out.append(
                send(
                    r4.at[n, :, h],
                    bmat.at[n, :, rows, :],
                    s5_send.at[n, h],
                    s5_recv.at[n, h],
                    device(x, zh, zl, second_partner[h], c),
                )
            )
            bmat[n, :, rows, :] = r4[n, :, h]
        return out

    def stage6(n, cps):
        out = []
        arrive(cps)
        for h in range(2):
            rows = pl.ds(aligned(h * 256 + half[h] * 128, 128), 128)
            out.append(
                send(
                    bmat.at[n, :, rows, :],
                    bmat.at[n, :, rows, :],
                    s6_send.at[n, h],
                    s6_recv.at[n, h],
                    device(x, zh, zl, first_partner[h], c),
                )
            )
        return out

    def product(n, rows):
        total = jnp.dot(hf[4, rows, :], bmat[n, x], preferred_element_type=F32)
        for at in range(4):
            total = total + jnp.dot(
                hf[at, rows, :], bmat[n, at], preferred_element_type=F32
            )
        return total

    a1 = stage1(0)
    a0 = to_other_core(0)
    a1 += stage1_rest(0, a0)
    own_blocks(0)
    for cp in scalar_loads:
        cp.wait()
    picks = []
    for h in range(2):
        row = []
        for k in range(2):
            o = owner_ref[0, k]
            pick = jnp.int32(4)
            sources = (
                zl * 8 + y * 2 + c,
                zl * 8 + y * 2 + oc,
                zl * 8 + first_partner[h] * 2 + c,
                zl * 8 + first_partner[h] * 2 + oc,
            )
            for at, source in enumerate(sources):
                pick = jnp.where(o == source, at, pick)
            row.append(pick)
        picks.append(row)

    place_rows()
    apply_inverse()
    a2 = stage2(0, a1)
    b1 = stage1(1)
    b0 = to_other_core(1)
    b1 += stage1_rest(1, b0)
    own_blocks(1)
    stage3(0, a2)
    fold_tiles(0, 3)
    fold_tiles(1, 1)
    nb_cps = [
        send(band.at[0:64], nb.at[1], nb_send.at[0], nb_recv.at[0], (sub, before)),
        send(band.at[192:256], nb.at[0], nb_send.at[1], nb_recv.at[1], (sub, after)),
    ]
    b2 = stage2(1, b1)
    stage4(0)
    arrive(nb_cps)
    for k in range(2):
        at = slice(k * 512, (k + 1) * 512)
        for part in range(2):
            rows = slice(part * 64, (part + 1) * 64)
            full = band[64 + part * 64 : 128 + part * 64, at] + nb[part, :, at]
            high = full.astype(BF16)
            hs[k, rows] = high
            low[k, rows] = (full - high.astype(F32)).astype(BF16)
    own_rows = pl.ds(aligned(c * 128, 128), 128)
    h_cps = []
    for a in range(1, 4):
        h_cps.append(
            send(
                hs.at[flip(x, a) // 2],
                hf.at[x, own_rows, :],
                h_send.at[a],
                h_recv.at[a],
                device(flip(x, a), zh, zl, y, c),
            )
        )
    hf[x, own_rows, :] = hs[x // 2]
    hf[4, own_rows, :] = low[x // 2]

    stage3(1, b2)
    a5 = stage5(0)
    stage4(1)
    a6 = stage6(0, a5)
    arrive(h_cps)
    h_cps = [
        send(
            hf.at[:, own_rows, :],
            hf.at[:, own_rows, :],
            h_send.at[0],
            h_recv.at[0],
            device(x, zh, zl, y, oc),
        )
    ]
    b5 = stage5(1)
    arrive(h_cps)
    arrive(a6)
    @pl.when(zh == 0)
    def _():
        pl.semaphore_wait(ready, 2)

    late_cps = []
    for d, core in enumerate((c, oc)):
        rows = pl.ds(aligned(core * 128, 128), 128)
        away[d] = product(0, rows).astype(BF16)
        late_cps.append(
            send(away.at[d], late.at[d], late_send.at[d], late_recv.at[d], opposites[d])
        )
    b6 = stage6(1, b5)
    arrive(b6)
    own = pl.ds(aligned(c * 128, 128), 128)
    other = pl.ds(aligned(oc * 128, 128), 128)
    pmat[...] = product(1, other)
    late_cps.append(
        send(pmat, cross, late_send.at[2], late_recv.at[2], device(x, zh, zl, y, oc))
    )
    mine = product(1, own)
    iface_load.wait()
    out_ref[:, own] = iface[:, own] - mine
    arrive(late_cps)
    out_ref[:, own] = out_ref[:, own] - late[0].astype(F32)
    out_ref[:, other] = iface[:, other] - (cross[...] + late[1].astype(F32))
    for cp in started:
        cp.wait_send()
    for n in range(2):

        @pl.when(mid == 0)
        def _():
            remote(
                m2.at[n, :, :, home_rows(1), :],
                r3.at[n, 2],
                s3_send.at[n, 1],
                s3_recv.at[n, 2],
                device(x, zh, zl, y, oc),
            ).wait_send()

        @pl.when(mid == 1)
        def _():
            for a in range(4):
                for b in range(4):
                    if a or b:
                        spread(n, a, b).wait_send()


def per_device(
    stretch_store,
    stretch_owner,
    tile_map,
    inverse_block,
    face_coupling,
    row_offset,
    row_count,
    interface_block,
):
    hbm = pl.BlockSpec(memory_space=pltpu.HBM)
    dma = pltpu.SemaphoreType.DMA
    return pl.pallas_call(
        kernel,
        out_shape=pltpu.VMEM((128, 256), F32),
        in_specs=[hbm] * 8,
        out_specs=pl.BlockSpec(memory_space=pltpu.VMEM),
        scratch_shapes=[
            pltpu.SMEM((1, 2), jnp.int32),
            pltpu.SMEM((1, 2, 2, 8), jnp.int32),
            pltpu.SMEM((1, 2), jnp.int32),
            pltpu.SMEM((1, 2), jnp.int32),
            pltpu.VMEM((2, 2, 2, 512, 128), BF16),
            pltpu.VMEM((2, 1024, 1024), BF16),
            pltpu.VMEM((2, 1024, 128), BF16),
            pltpu.VMEM((128, 256), F32),
            pltpu.VMEM((2, 5, 2, 128, 128), BF16),
            pltpu.VMEM((2, 5, 2, 128, 128), BF16),
            pltpu.VMEM((2, 2, 2, 128, 128), BF16),
            pltpu.VMEM((2, 2, 4, 64, 128), BF16),
            pltpu.VMEM((2, 2, 4, 64, 128), BF16),
            pltpu.VMEM((2, 2, 4, 64, 128), BF16),
            pltpu.VMEM((2, 3, 2, 4, 32, 128), BF16),
            pltpu.VMEM((2, 2, 4, 32, 128), BF16),
            pltpu.VMEM((2, 4, 2, 64, 128), BF16),
            pltpu.VMEM((2, 4, 512, 128), BF16),
            pltpu.VMEM((2, 256, 1024), BF16),
            pltpu.VMEM((2, 256, 1024), F32),
            pltpu.VMEM((256, 1024), F32),
            pltpu.VMEM((2, 64, 1024), F32),
            pltpu.VMEM((2, 128, 512), BF16),
            pltpu.VMEM((2, 128, 512), BF16),
            pltpu.VMEM((5, 256, 512), BF16),
            pltpu.VMEM((128, 128), F32),
            pltpu.VMEM((2, 128, 128), BF16),
            pltpu.VMEM((2, 128, 128), BF16),
            pltpu.VMEM((128, 128), F32),
            dma((16,)),
            dma((2, 2)),
            dma((2, 2)),
            dma((2, 2, 3)),
            dma((2, 2, 3)),
            dma((2, 2)),
            dma((2, 2)),
            dma((2, 2)),
            dma((2, 3)),
            dma((2, 4, 4)),
            dma((2, 4, 2)),
            dma((2, 2)),
            dma((2, 2)),
            dma((2, 2)),
            dma((2, 2)),
            dma((2,)),
            dma((2,)),
            dma((4,)),
            dma((4,)),
            dma((3,)),
            dma((3,)),
            pltpu.SemaphoreType.REGULAR,
        ],
        compiler_params=pltpu.CompilerParams(
            collective_id=0, has_side_effects=True, vmem_limit_bytes=40 * 1024 * 1024
        ),
        name="schur",
    )(
        *(
            pltpu.with_memory_space_constraint(operand, pltpu.HBM)
            for operand in (
                stretch_owner,
                tile_map,
                row_offset,
                row_count,
                stretch_store,
                inverse_block,
                face_coupling,
                interface_block,
            )
        )
    )


def solution(mesh):
    return jax.shard_map(
        per_device,
        mesh=mesh,
        in_specs=(
            P("sub", "ifc", None, None),
            P("sub", None),
            P("sub", "ifc", None, None),
            P("sub", "ifc", None, None),
            P("sub", "ifc", None, None),
            P("sub", "ifc"),
            P("sub", "ifc"),
            P("ifc", "sub"),
        ),
        out_specs=P("ifc", "sub"),
        check_vma=False,
    )
```

```python
import jax
import jax.numpy as jnp
from jax import lax
from jax.experimental import pallas as pl
from jax.experimental.pallas import tpu as pltpu
from jax.sharding import PartitionSpec as P

MESH = pl.DeviceIdType.MESH
F32 = jnp.float32
BF16 = jnp.bfloat16
NT_DIMS = (((1,), (1,)), ((), ()))


def aligned(value, unit):
    return pl.multiple_of(value, unit)


def kernel(
    owner_hbm,
    map_hbm,
    offset_hbm,
    count_hbm,
    store_ref,
    inverse_ref,
    face_ref,
    iface_ref,
    out_ref,
    owner_ref,
    map_ref,
    offset_ref,
    count_ref,
    st,
    inv,
    face,
    iface,
    r1_first,
    r1_second,
    so,
    s2,
    r2,
    m2,
    r3,
    m3,
    r4,
    bmat,
    placed,
    gband,
    band,
    nb,
    hs,
    low,
    hf,
    pmat,
    away,
    late,
    cross,
    load_sem,
    s0_send,
    s0_recv,
    s1_send,
    s1_recv,
    s2_send,
    s2_recv,
    s3_send,
    s3_recv,
    s4_send,
    s4_recv,
    s5_send,
    s5_recv,
    s6_send,
    s6_recv,
    nb_send,
    nb_recv,
    h_send,
    h_recv,
    late_send,
    late_recv,
    ready,
):
    sub = lax.axis_index("sub")
    ifc = lax.axis_index("ifc")
    x, zh = sub // 2, sub % 2
    zl, y, c = ifc // 8, (ifc // 2) % 4, ifc % 2

    def flip(value, mask):
        out = 0
        for bit in (1, 2):
            digit = (value // bit) % 2
            out = out + bit * ((1 - digit) if mask & bit else digit)
        return out

    def device(x_, zh_, zl_, y_, c_):
        return (x_ * 2 + zh_, zl_ * 8 + y_ * 2 + c_)

    oc = 1 - c
    r1 = (r1_first, r1_second)
    first_partner = (flip(y, 1), flip(y, 3))
    second_partner = (flip(y, 3), flip(y, 1))
    y0, y1 = y % 2, y // 2
    half = ((y0 + y1) % 2, y1)
    quarter = (y1, y0)

    partners = [device(x, zh, zl, y, oc)]
    for h in range(2):
        partners.append(device(x, zh, zl, first_partner[h], c))
    for a in range(4):
        for b in range(3):
            if a or b:
                partners.append(device(flip(x, a), zh, flip(zl, b), y, c))
    before, after = lax.rem(ifc + 31, 32), lax.rem(ifc + 1, 32)
    partners.append((sub, lax.rem(ifc + 31 + 2 * c, 32)))
    mid = (zl // 2 + zl) % 2
    steps = ((1 - zh), zh)
    strips = ([], [])

    def load_strips(n):
        for xh in range(2):
            for cc in range(2):
                at = aligned(xh * 512 + steps[n] * 256 + cc * 128, 128)
                cp = pltpu.make_async_copy(
                    store_ref.at[0, 0, :, pl.ds(at, 128)],
                    st.at[n, xh, cc],
                    load_sem.at[n * 4 + xh * 2 + cc],
                )
                cp.start()
                strips[n].append(cp)

    load_strips(0)
    barrier = pltpu.get_barrier_semaphore()
    for partner in partners:
        pl.semaphore_signal(barrier, inc=1, device_id=partner, device_id_type=MESH)

    @pl.when(mid == 1)
    def _():
        for a in range(4):
            pl.semaphore_signal(
                barrier,
                inc=1,
                device_id=device(flip(x, a), zh, 3 - zl, y, c),
                device_id_type=MESH,
            )


    load_strips(1)
    scalar_loads = []
    for at, (src, dst) in enumerate(
        (
            (owner_hbm, owner_ref),
            (map_hbm, map_ref),
            (offset_hbm, offset_ref),
            (count_hbm, count_ref),
        )
    ):
        cp = pltpu.make_async_copy(src, dst, load_sem.at[8 + at])
        cp.start()
        scalar_loads.append(cp)
    face_load = pltpu.make_async_copy(face_ref.at[0], face, load_sem.at[12])
    face_load.start()
    inv_loads = []
    for l in range(2):
        cp = pltpu.make_async_copy(inverse_ref.at[0, l], inv.at[l], load_sem.at[13 + l])
        cp.start()
        inv_loads.append(cp)
    iface_load = pltpu.make_async_copy(iface_ref, iface, load_sem.at[15])
    iface_load.start()

    def place_rows():
        face_load.wait()
        row_at = lax.broadcasted_iota(jnp.int32, (256, 128), 0)
        col_at = lax.broadcasted_iota(jnp.int32, (256, 128), 1)
        for l in range(2):
            start = offset_ref[0, l] - (ifc * 128 - 64)
            here = jnp.logical_and(row_at == col_at + start, col_at < count_ref[0, l])
            place = jnp.where(here, 1.0, 0.0).astype(BF16)
            placed[l] = lax.dot_general(
                place, face[l], NT_DIMS, preferred_element_type=F32
            ).astype(BF16)

    def apply_inverse():
        for l in range(2):
            inv_loads[l].wait()

            def columns(i, _):
                at = pl.ds(aligned(i * 256, 256), 256)
                gband[l, :, at] = jnp.dot(
                    placed[l], inv[l, :, at], preferred_element_type=F32
                )
                return 0

            lax.fori_loop(0, 4, columns, 0)

    def fold_tiles(first, step):
        def fold(r, _):
            rows = pl.ds(aligned((first + r * step) * 64, 64), 64)
            for k in range(2):
                accs = [jnp.zeros((64, 128), F32) for _ in range(4)]
                for l in range(2):
                    for i in range(8):
                        block = gband[l, rows, i * 128 : (i + 1) * 128]
                        tile = map_ref[0, l, k, i]
                        for t in range(4):
                            accs[t] = accs[t] + jnp.where(tile == t, 1.0, 0.0) * block
                for t in range(4):
                    at = k * 512 + t * 128
                    band[rows, at : at + 128] = accs[t]
            return 0

        lax.fori_loop(0, 2, fold, 0)

    def kept(h):
        return pl.ds(aligned(h * 256 + half[h] * 128, 128), 128)

    def given(h):
        return pl.ds(aligned(h * 256 + (1 - half[h]) * 128, 128), 128)

    def own_blocks(n):
        for h in range(2):
            r1[n][h, 0] = st[n, :, c, kept(h), :]
            r1[n][h, 4] = jnp.zeros((2, 128, 128), BF16)

    started = []

    def home_rows(home):
        return pl.ds(aligned((home - 1) * 32, 32), 32)

    def remote(src, dst, send_sem, recv_sem, to):
        return pltpu.make_async_remote_copy(
            src_ref=src,
            dst_ref=dst,
            send_sem=send_sem,
            recv_sem=recv_sem,
            device_id=to,
            device_id_type=MESH,
        )

    def send(src, dst, send_sem, recv_sem, to):
        cp = remote(src, dst, send_sem, recv_sem, to)
        cp.start()
        started.append(cp)
        return cp

    got = []

    def arrive(cps):
        for cp in cps:
            cp.wait_recv()
            got.append(cp)

    opposite = device(x, 1 - zh, zl, y, c)
    pl.semaphore_wait(barrier, len(partners) + 2 * zh + 4 * mid)

    opposites = (opposite, device(x, 1 - zh, zl, y, oc))

    @pl.when(zh == 0)
    def _():
        for to in opposites:
            pl.semaphore_signal(barrier, inc=1, device_id=to, device_id_type=MESH)

    @pl.when(zh == 1)
    def _():
        for to in opposites:
            pl.semaphore_signal(ready, inc=1, device_id=to, device_id_type=MESH)


    def to_other_core(n):
        out = []
        for h in range(2):
            out.append(
                send(
                    st.at[n, :, oc, given(h), :],
                    so.at[n, h],
                    s0_send.at[n, h],
                    s0_recv.at[n, h],
                    device(x, zh, zl, y, oc),
                )
            )
        return out

    def stage1(n):
        out = []
        for cp in strips[n]:
            cp.wait()
        for h in range(2):
            out.append(
                send(
                    st.at[n, :, c, given(h), :],
                    r1[n].at[h, 2],
                    s1_send.at[n, h, 0],
                    s1_recv.at[n, h, 0],
                    device(x, zh, zl, first_partner[h], c),
                )
            )
        return out

    def stage1_rest(n, cps):
        out = []
        arrive(cps)
        for h in range(2):
            out.append(
                send(
                    so.at[n, h],
                    r1[n].at[h, 3],
                    s1_send.at[n, h, 1],
                    s1_recv.at[n, h, 1],
                    device(x, zh, zl, first_partner[h], c),
                )
            )
        for h in range(2):
            out.append(
                send(
                    st.at[n, :, oc, kept(h), :],
                    r1[n].at[h, 1],
                    s1_send.at[n, h, 2],
                    s1_recv.at[n, h, 2],
                    device(x, zh, zl, y, oc),
                )
            )
        return out

    def stage2(n, cps):
        out = []
        arrive(cps)
        for h in range(2):
            rows = pl.ds(aligned((1 - quarter[h]) * 64, 64), 64)
            for k in range(2):
                s2[n, h, 2 * k : 2 * k + 2] = r1[n][h, picks[h][k], :, rows, :]
            out.append(
                send(
                    s2.at[n, h],
                    r2.at[n, h],
                    s2_send.at[n, h],
                    s2_recv.at[n, h],
                    device(x, zh, zl, second_partner[h], c),
                )
            )
        return out

    def stage3(n, cps):
        arrive(cps)
        for h in range(2):
            rows = pl.ds(aligned(quarter[h] * 64, 64), 64)
            for k in range(2):
                m2[n, h, 2 * k : 2 * k + 2] = (
                    r1[n][h, picks[h][k], :, rows, :] + r2[n, h, 2 * k : 2 * k + 2]
                )
        a_home, b_home = 1 + zl % 2, 2 - zl % 2
        send(
            m2.at[n, :, :, home_rows(a_home), :],
            r3.at[n, mid],
            s3_send.at[n, 0],
            s3_recv.at[n, mid],
            device(x, zh, a_home, y, c),
        )

        @pl.when(mid == 0)
        def _():
            remote(
                m2.at[n, :, :, home_rows(b_home), :],
                r3.at[n, 2],
                s3_send.at[n, 1],
                s3_recv.at[n, 2],
                device(x, zh, b_home, y, c),
            ).start()

    def spread(n, a, b):
        return remote(
            m3.at[n, :, flip(x, a)],
            r4.at[n, x, :, home_rows(zl), :],
            s4_send.at[n, a, b],
            s4_recv.at[n, a, zl - 1],
            device(flip(x, a), zh, flip(zl, b), y, c),
        )

    def stage4(n):
        @pl.when(mid == 1)
        def _():
            for slot in range(3):
                remote(
                    r3.at[n, slot],
                    r3.at[n, slot],
                    s3_send.at[n, 0],
                    s3_recv.at[n, slot],
                    device(x, zh, zl, y, oc),
                ).wait_recv()
            m3[n] = (
                m2[n, :, :, home_rows(zl), :] + r3[n, 0] + r3[n, 1] + r3[n, 2]
            )
            for b in (2, 3, 1, 0):
                for a in (2, 1, 3, 0):
                    if a or b:
                        spread(n, a, b).start()
            r4[n, x, :, home_rows(zl), :] = m3[n, :, x]

    def from_home(n, a, home):
        rows = home_rows(home)
        remote(
            r4.at[n, flip(x, a), :, rows, :],
            r4.at[n, flip(x, a), :, rows, :],
            s4_send.at[n, 0, 0],
            s4_recv.at[n, a, home - 1],
            device(x, zh, zl, y, oc),
        ).wait_recv()

    def stage5(n):
        from_home(n, 0, 1 + mid * (2 - zl))
        for a in range(1, 4):
            for home in (1, 2):
                from_home(n, a, home)

        @pl.when(mid == 0)
        def _():
            from_home(n, 0, 2)

        out = []
        for h in range(2):
            rows = pl.ds(aligned(h * 256 + half[h] * 128 + quarter[h] * 64, 64), 64)
            out.append(
                send(
                    r4.at[n, :, h],
                    bmat.at[n, :, rows, :],
                    s5_send.at[n, h],
                    s5_recv.at[n, h],
                    device(x, zh, zl, second_partner[h], c),
                )
            )
            bmat[n, :, rows, :] = r4[n, :, h]
        return out

    def stage6(n, cps):
        out = []
        arrive(cps)
        for h in range(2):
            rows = pl.ds(aligned(h * 256 + half[h] * 128, 128), 128)
            out.append(
                send(
                    bmat.at[n, :, rows, :],
                    bmat.at[n, :, rows, :],
                    s6_send.at[n, h],
                    s6_recv.at[n, h],
                    device(x, zh, zl, first_partner[h], c),
                )
            )
        return out

    def product(n, rows):
        total = jnp.dot(hf[4, rows, :], bmat[n, x], preferred_element_type=F32)
        for at in range(4):
            total = total + jnp.dot(
                hf[at, rows, :], bmat[n, at], preferred_element_type=F32
            )
        return total

    a1 = stage1(0)
    a0 = to_other_core(0)
    a1 += stage1_rest(0, a0)
    own_blocks(0)
    for cp in scalar_loads:
        cp.wait()
    picks = []
    for h in range(2):
        row = []
        for k in range(2):
            o = owner_ref[0, k]
            pick = jnp.int32(4)
            sources = (
                zl * 8 + y * 2 + c,
                zl * 8 + y * 2 + oc,
                zl * 8 + first_partner[h] * 2 + c,
                zl * 8 + first_partner[h] * 2 + oc,
            )
            for at, source in enumerate(sources):
                pick = jnp.where(o == source, at, pick)
            row.append(pick)
        picks.append(row)

    place_rows()
    apply_inverse()
    a2 = stage2(0, a1)
    b1 = stage1(1)
    b0 = to_other_core(1)
    b1 += stage1_rest(1, b0)
    own_blocks(1)
    stage3(0, a2)
    fold_tiles(0, 3)
    fold_tiles(1, 1)
    nb_cps = [
        send(band.at[0:64], nb.at[1], nb_send.at[0], nb_recv.at[0], (sub, before)),
        send(band.at[192:256], nb.at[0], nb_send.at[1], nb_recv.at[1], (sub, after)),
    ]
    b2 = stage2(1, b1)
    stage4(0)
    arrive(nb_cps)
    for k in range(2):
        at = slice(k * 512, (k + 1) * 512)
        for part in range(2):
            rows = slice(part * 64, (part + 1) * 64)
            full = band[64 + part * 64 : 128 + part * 64, at] + nb[part, :, at]
            high = full.astype(BF16)
            hs[k, rows] = high
            low[k, rows] = (full - high.astype(F32)).astype(BF16)
    own_rows = pl.ds(aligned(c * 128, 128), 128)
    h_cps = []
    for a in range(1, 4):
        h_cps.append(
            send(
                hs.at[flip(x, a) // 2],
                hf.at[x, own_rows, :],
                h_send.at[a],
                h_recv.at[a],
                device(flip(x, a), zh, zl, y, c),
            )
        )
    hf[x, own_rows, :] = hs[x // 2]
    hf[4, own_rows, :] = low[x // 2]

    def share(at, slot):
        return send(
            hf.at[at, own_rows, :],
            hf.at[at, own_rows, :],
            h_send.at[slot],
            h_recv.at[slot],
            device(x, zh, zl, y, oc),
        )

    shared = [share(x, 0), share(4, 7)]

    stage3(1, b2)
    a5 = stage5(0)
    stage4(1)
    a6 = stage6(0, a5)
    for a, cp in enumerate(h_cps, 1):
        arrive([cp])
        shared.append(share(flip(x, a), 3 + a))
    h_cps = shared
    b5 = stage5(1)
    arrive(h_cps)
    arrive(a6)
    @pl.when(zh == 0)
    def _():
        pl.semaphore_wait(ready, 2)

    late_cps = []
    for d, core in enumerate((c, oc)):
        rows = pl.ds(aligned(core * 128, 128), 128)
        away[d] = product(0, rows).astype(BF16)
        late_cps.append(
            send(away.at[d], late.at[d], late_send.at[d], late_recv.at[d], opposites[d])
        )
    b6 = stage6(1, b5)
    arrive(b6)
    own = pl.ds(aligned(c * 128, 128), 128)
    other = pl.ds(aligned(oc * 128, 128), 128)
    pmat[...] = product(1, other)
    late_cps.append(
        send(pmat, cross, late_send.at[2], late_recv.at[2], device(x, zh, zl, y, oc))
    )
    mine = product(1, own)
    iface_load.wait()
    out_ref[:, own] = iface[:, own] - mine
    arrive(late_cps)
    out_ref[:, own] = out_ref[:, own] - late[0].astype(F32)
    out_ref[:, other] = iface[:, other] - (cross[...] + late[1].astype(F32))
    for cp in started:
        cp.wait_send()
    for n in range(2):

        @pl.when(mid == 0)
        def _():
            remote(
                m2.at[n, :, :, home_rows(1), :],
                r3.at[n, 2],
                s3_send.at[n, 1],
                s3_recv.at[n, 2],
                device(x, zh, zl, y, oc),
            ).wait_send()

        @pl.when(mid == 1)
        def _():
            for a in range(4):
                for b in range(4):
                    if a or b:
                        spread(n, a, b).wait_send()


def per_device(
    stretch_store,
    stretch_owner,
    tile_map,
    inverse_block,
    face_coupling,
    row_offset,
    row_count,
    interface_block,
):
    hbm = pl.BlockSpec(memory_space=pltpu.HBM)
    dma = pltpu.SemaphoreType.DMA
    return pl.pallas_call(
        kernel,
        out_shape=pltpu.VMEM((128, 256), F32),
        in_specs=[hbm] * 8,
        out_specs=pl.BlockSpec(memory_space=pltpu.VMEM),
        scratch_shapes=[
            pltpu.SMEM((1, 2), jnp.int32),
            pltpu.SMEM((1, 2, 2, 8), jnp.int32),
            pltpu.SMEM((1, 2), jnp.int32),
            pltpu.SMEM((1, 2), jnp.int32),
            pltpu.VMEM((2, 2, 2, 512, 128), BF16),
            pltpu.VMEM((2, 1024, 1024), BF16),
            pltpu.VMEM((2, 1024, 128), BF16),
            pltpu.VMEM((128, 256), F32),
            pltpu.VMEM((2, 5, 2, 128, 128), BF16),
            pltpu.VMEM((2, 5, 2, 128, 128), BF16),
            pltpu.VMEM((2, 2, 2, 128, 128), BF16),
            pltpu.VMEM((2, 2, 4, 64, 128), BF16),
            pltpu.VMEM((2, 2, 4, 64, 128), BF16),
            pltpu.VMEM((2, 2, 4, 64, 128), BF16),
            pltpu.VMEM((2, 3, 2, 4, 32, 128), BF16),
            pltpu.VMEM((2, 2, 4, 32, 128), BF16),
            pltpu.VMEM((2, 4, 2, 64, 128), BF16),
            pltpu.VMEM((2, 4, 512, 128), BF16),
            pltpu.VMEM((2, 256, 1024), BF16),
            pltpu.VMEM((2, 256, 1024), F32),
            pltpu.VMEM((256, 1024), F32),
            pltpu.VMEM((2, 64, 1024), F32),
            pltpu.VMEM((2, 128, 512), BF16),
            pltpu.VMEM((2, 128, 512), BF16),
            pltpu.VMEM((5, 256, 512), BF16),
            pltpu.VMEM((128, 128), F32),
            pltpu.VMEM((2, 128, 128), BF16),
            pltpu.VMEM((2, 128, 128), BF16),
            pltpu.VMEM((128, 128), F32),
            dma((16,)),
            dma((2, 2)),
            dma((2, 2)),
            dma((2, 2, 3)),
            dma((2, 2, 3)),
            dma((2, 2)),
            dma((2, 2)),
            dma((2, 2)),
            dma((2, 3)),
            dma((2, 4, 4)),
            dma((2, 4, 2)),
            dma((2, 2)),
            dma((2, 2)),
            dma((2, 2)),
            dma((2, 2)),
            dma((2,)),
            dma((2,)),
            dma((8,)),
            dma((8,)),
            dma((3,)),
            dma((3,)),
            pltpu.SemaphoreType.REGULAR,
        ],
        compiler_params=pltpu.CompilerParams(
            collective_id=0, has_side_effects=True, vmem_limit_bytes=40 * 1024 * 1024
        ),
        name="schur",
    )(
        *(
            pltpu.with_memory_space_constraint(operand, pltpu.HBM)
            for operand in (
                stretch_owner,
                tile_map,
                row_offset,
                row_count,
                stretch_store,
                inverse_block,
                face_coupling,
                interface_block,
            )
        )
    )


def solution(mesh):
    return jax.shard_map(
        per_device,
        mesh=mesh,
        in_specs=(
            P("sub", "ifc", None, None),
            P("sub", None),
            P("sub", "ifc", None, None),
            P("sub", "ifc", None, None),
            P("sub", "ifc", None, None),
            P("sub", "ifc"),
            P("sub", "ifc"),
            P("ifc", "sub"),
        ),
        out_specs=P("ifc", "sub"),
        check_vma=False,
    )
```
